32 devices in a mesh: groups: 2 (over x), tensor: 8 (over z, y), role: 2 (over core).
Axes of the slice: x: 2, y: 2, z: 4, core: 2. Of those that a mesh axis runs over, the one named last changes fastest.
Arguments:
- context: bfloat16 [320, 8192], P('groups', ('tensor', 'role')), parts along dimension 0, may hold values from -6 to 6
- w_out: bfloat16 [8192, 8192], P(('tensor', 'role')), may hold values from -0.09375 to 0.09375
- residual: bfloat16 [320, 8192], P('groups', ('tensor', 'role')), parts along dimension 0, may hold values from -6 to 6
- fc_rest: bfloat16 [320, 8192], P('groups', ('tensor', 'role')), parts along dimension 0, may hold values from -6 to 6
- w_fc: bfloat16 [8192, 8192], P(None, ('tensor', 'role')), may hold values from -0.0625 to 0.0625
- norm_gain: float32 [8192], P(('tensor', 'role')), may hold values from 0.25 to 1.75
- w_lm: bfloat16 [8192, 16000], P(None, ('tensor', 'role')), may hold values from -0.0625 to 0.0625
- tokens: int32 [324], P('groups'), parts along dimension 0, may hold values from 0 to 128255
- segments: int32 [324], P('groups'), parts along dimension 0, may hold values from 0 to 3, never falling along the last dimension, each value on 1 to 80 neighbouring positions
- vocab_map: int32 [256512], P('groups'), parts along dimension 0, may hold values from -1 to 15999, as said below
Outputs:
- step_losses: float32 [4], P('groups'), parts along dimension 0
- grad_fc: bfloat16 [16384, 8192], P('groups', ('tensor', 'role')), parts along dimension 0
- grad_gain: float32 [16384], P(('groups', 'tensor', 'role')), parts along dimension 0
The draws below stay inside these ranges and needn't reach their ends.
There are 2 independent parts, one for each index of `groups`. The reference program is written for one: setup_inputs(seed, part) draws one part's arguments, and reference() takes and returns one part's arrays. A program takes and returns all parts, laid end to end along the dimension named above; an argument that names none is the same for every part. Nothing has to cross between parts.
Inputs may be any that keep to these rules, and one draw needn't show every extreme that they name: `vocab_map`: each draft id 0 to 15999 appears exactly once; all other entries are -1.
All inputs are finite; a program needn't handle non-finite values.
Results may differ from the reference program's by a relative error of at most 0.0058.
Values may be sent and summed in bfloat16 or wider, within the bound.
A program may use at most 128 MiB of HBM per device.

```python
import math
import jax
import jax.numpy as jnp
import numpy as np
from jax import lax

D = 8192
H = 64
HD = 128
TV = 128256
V = 16000
TOK = 160


def pairing(key):
    return jax.random.permutation(key, TV).astype(jnp.int32)


def draw_vocab_map(key, part):
    shuffled = pairing(key)
    return jnp.where(shuffled < V, shuffled, -1).astype(jnp.int32)


def draw_tokens(key, part):
    shuffled = pairing(key)
    key = jax.random.fold_in(key, 7)
    inverse = jnp.argsort(shuffled)[:V].astype(jnp.int32)
    first, second, third = jax.random.split(key, 3)
    drafted = jax.random.randint(first, (TOK + 2,), 0, V)
    others = jax.random.randint(second, (TOK + 2,), 0, TV)
    keeper = jax.random.randint(third, (TOK + 2,), 0, 4) > 0
    return jnp.where(keeper, inverse[drafted], others).astype(jnp.int32)


def spiked(entries, key, source, target, blocks, factor):
    def block_of(dim):
        return (jnp.arange(entries.shape[dim]) // (entries.shape[dim] // blocks)).reshape((-1,) + (1,) * (entries.ndim - 1 - dim))

    near = jax.random.permutation(key, blocks)[block_of(target)]
    other_side = (block_of(target) + blocks // 2) % blocks
    return jnp.where((block_of(source) == near) | (block_of(source) == other_side), factor * entries, entries)


def block_scale(key, shape, pieces, low, high):
    def one(axis_at, blocks):
        steps = jax.random.uniform(jax.random.fold_in(jax.random.fold_in(key, 6), axis_at), (blocks,), jnp.float32, low / len(pieces), high / len(pieces))
        return jnp.repeat(jnp.exp(steps), shape[axis_at] // blocks).reshape((-1,) + (1,) * (len(shape) - axis_at - 1))

    level = one(*pieces[0])
    for cut in pieces[1:]:
        level = level * one(*cut)
    return level


def split_up(amount, total, reach, lean):
    weights = [(1 << 20) // math.isqrt(standing ** lean) + 1 for standing in range(2, amount + 1)]
    surplus, holding = total - reach - (amount - 1), [1] * (amount - 1)
    while surplus > 0:
        free = [i for i in range(amount - 1) if holding[i] < reach]
        pool, remaining = sum([weights[i] for i in free]), surplus
        for i in free:
            extra = min(reach - holding[i], max(1, remaining * weights[i] // pool), surplus)
            holding[i] = holding[i] + extra
            surplus = surplus - extra
    return np.array([reach] + holding)


def ragged_sizes(key, count, total, bound, skew):
    if count == 2:
        one = jax.random.randint(key, (), max(1, total - bound), min(bound, total - 1) + 1)
        return jnp.stack([one, total - one])
    sizes = jnp.asarray(split_up(count, total, bound, skew), jnp.int32)
    couples = (count - 1) // 2
    giver, sink = sizes[1:1 + 2 * couples:2], sizes[2:2 + 2 * couples:2]
    margin = jnp.minimum(giver - 1, bound - sink)
    passed = jax.random.randint(jax.random.fold_in(key, 1), (couples,), 0, 1 << 20) % (margin + 1)
    sizes = sizes.at[1:1 + 2 * couples:2].set(giver - passed).at[2:2 + 2 * couples:2].set(sink + passed)
    return sizes[jax.random.permutation(jax.random.fold_in(key, 2), count)]


def centred(stream_key, extent, spread, most, pieces=(), kind=jnp.bfloat16):
    values = spread * jax.random.normal(stream_key, extent, jnp.float32)
    if pieces:
        values = values * block_scale(stream_key, extent, pieces, -0.22, 0.18)
    return jnp.clip(values, -most, most).astype(kind)


def gaussian_with(rng, dims, deviation, reach, cuts, heavy, kind=jnp.bfloat16):
    array = deviation * jax.random.normal(rng, dims, jnp.float32)
    if cuts:
        array = array * block_scale(rng, dims, cuts, -0.22, 0.18)
    return jnp.clip(spiked(array, jax.random.fold_in(rng, 3), *heavy), -reach, reach).astype(kind)


def setup_inputs(seed: int = 0, part: int = 0) -> dict:
    key_of = jax.random.split(jax.random.key(seed), 11)
    part_splits = jax.random.split(jax.random.fold_in(key_of[10], part), 11)
    return {
        "context": centred(part_splits[0], (TOK, H * HD), 1.0, 6.0, ((1, 16),)),
        "w_out": gaussian_with(key_of[1], (H * HD, D), (H * HD) ** -0.5, 0.09375, ((0, 16),), (0, 1, 16, 2.0)),
        "residual": centred(part_splits[2], (TOK, D), 1.0, 6.0, ((1, 16),)),
        "fc_rest": centred(part_splits[3], (TOK, D), 1.0, 6.0, ((1, 16),)),
        "w_fc": centred(key_of[4], (D, D), D ** -0.5, 0.0625, ((1, 16),)),
        "norm_gain": jnp.clip(1.0 + 0.15 * jax.random.normal(key_of[5], (D,), jnp.float32), 0.25, 1.75),
        "w_lm": centred(key_of[6], (D, V), D ** -0.5, 0.0625, ((1, 16),)),
        "tokens": draw_tokens(jax.random.fold_in(jax.random.fold_in(key_of[10], part), 71), part),
        "segments": jnp.searchsorted(jnp.cumsum(ragged_sizes(part_splits[8], 4, TOK + 2, TOK // 2, 1)), jnp.arange(TOK + 2), side="right").astype(jnp.int32),
        "vocab_map": draw_vocab_map(jax.random.fold_in(jax.random.fold_in(key_of[10], part), 71), part),
    }


EPS = 1e-05

def settle(state, norm_gain):
    inverse = lax.rsqrt(lax.optimization_barrier(jnp.mean(state * state, axis=1)) + EPS)
    return ((state * inverse[:, None] * norm_gain).astype(jnp.bfloat16), inverse)

def unwind(state, inverse, grad_normed, norm_gain):
    scaled = norm_gain * grad_normed
    projection = lax.optimization_barrier(jnp.mean(state * scaled, axis=1))
    grad_state = inverse[:, None] * scaled - state * (inverse ** 3 * projection)[:, None]
    gain_grad = lax.optimization_barrier(jnp.sum(grad_normed * state * inverse[:, None], axis=0))
    return (grad_state, gain_grad)

def reference(context, w_out, residual, fc_rest, w_fc, norm_gain, w_lm, tokens, segments, vocab_map):
    captured = (jnp.dot(context, w_out, preferred_element_type=jnp.float32) + residual.astype(jnp.float32)).astype(jnp.bfloat16)
    features = fc_rest.astype(jnp.float32) + jnp.dot(captured, w_fc, preferred_element_type=jnp.float32)
    seg_now = segments[:TOK]
    follows = jnp.concatenate([jnp.zeros((1,), jnp.float32), (segments[1:TOK] == segments[:TOK - 1]).astype(jnp.float32)])
    normed_one, scale_one = settle(features, norm_gain)
    shifted = jnp.concatenate([jnp.zeros((1, D), jnp.float32), normed_one[:-1].astype(jnp.float32)], axis=0)
    second = features + shifted * follows[:, None]
    normed_two, scale_two = settle(second, norm_gain)
    columns = jnp.arange(V, dtype=jnp.int32)

    def head(normed, shift, weight):
        labels = vocab_map[tokens[shift:shift + TOK]]
        usable = ((labels >= 0) & (segments[shift:shift + TOK] == seg_now)).astype(jnp.float32)
        logits = jnp.dot(normed, w_lm, preferred_element_type=jnp.float32)
        powers = jnp.exp(logits)
        totals = lax.optimization_barrier(jnp.sum(powers, axis=1))
        matches = columns[None, :] == labels[:, None]
        picked = lax.optimization_barrier(jnp.sum(jnp.where(matches, logits, 0.0), axis=1))
        average = jnp.sum(usable * (jnp.log(totals) - picked)) / jnp.maximum(jnp.sum(usable), 1.0)
        dlogits = ((weight * usable)[:, None] * (powers / totals[:, None] - matches.astype(jnp.float32))).astype(jnp.bfloat16)
        head_grad = jnp.dot(dlogits, w_lm.T, preferred_element_type=jnp.float32)
        return (average, head_grad)
    loss_one, head_one = head(normed_one, 1, 1.0)
    loss_two, head_two = head(normed_two, 2, 0.8)
    grad_two, gain_two = unwind(second, scale_two, head_two, norm_gain)
    carried = head_one + jnp.concatenate([grad_two[1:] * follows[1:, None], jnp.zeros((1, D), jnp.float32)], axis=0)
    grad_one, gain_one = unwind(features, scale_one, carried, norm_gain)
    grad_fc = jnp.dot(captured.T, (grad_one + grad_two).astype(jnp.bfloat16), preferred_element_type=jnp.float32).astype(jnp.bfloat16)
    return (jnp.stack([loss_one, loss_two]), grad_fc, gain_one + gain_two)
```

```python
import functools

import jax
import jax.numpy as jnp
from jax import lax
from jax.experimental import pallas as pl
from jax.experimental.pallas import tpu as pltpu
from jax.sharding import PartitionSpec as P

EPS = 1e-05
SHRINK = 1.0 / 1024.0
VMEM_BYTES = 56 * 1024 * 1024
EXTRA = 16
MESH = pl.DeviceIdType.MESH


def in_vmem():
    return pl.BlockSpec(memory_space=pltpu.VMEM)


def product(a, b):
    return jnp.dot(a, b, preferred_element_type=jnp.float32)


def greet(tensors, t, r):
    barrier = pltpu.get_barrier_semaphore()

    def hello(k, _):
        pl.semaphore_signal(
            barrier, inc=1, device_id={"tensor": lax.rem(t + k, tensors)}, device_id_type=MESH
        )
        return 0

    lax.fori_loop(1, tensors, hello, 0)
    pl.semaphore_signal(barrier, inc=1, device_id={"role": 1 - r}, device_id_type=MESH)
    pl.semaphore_wait(barrier, tensors)


def to_peer(src, dst, send_sem, recv_sem, peer):
    return pltpu.make_async_remote_copy(
        src_ref=src, dst_ref=dst, send_sem=send_sem, recv_sem=recv_sem,
        device_id={"tensor": peer}, device_id_type=MESH,
    )


def to_sibling(src, dst, send_sem, recv_sem, r):
    return pltpu.make_async_remote_copy(
        src_ref=src, dst_ref=dst, send_sem=send_sem, recv_sem=recv_sem,
        device_id={"role": 1 - r}, device_id_type=MESH,
    )


def scatter_sum(tensors, t, r, part, narrow, bufs, sems, total):
    pair_out, pair_in, out, inn = bufs
    pair_send, pair_recv, send, recv = sems

    def pair(d):
        return to_sibling(pair_out.at[d], pair_in.at[d], pair_send.at[d], pair_recv.at[d], r)

    def ahead(d):
        pair_out[d] = part(2 * d + 1 - r)
        pair(d).start()

    ahead(lax.rem(t + 1, tensors))

    def step(k, _):
        d = lax.rem(t + 1 + k, tensors)
        ahead(lax.rem(t + 2 + k, tensors))
        own = part(2 * d + r)
        pair(d).wait_recv()
        out[d] = narrow(own + pair_in[d])
        to_peer(out.at[d], inn.at[t], send.at[d], recv.at[t], d).start()
        return 0

    lax.fori_loop(0, tensors - 1, step, 0)
    own = part(2 * t + r)
    pair(t).wait_recv()
    total[...] = own + pair_in[t]

    def collect(k, _):
        s = lax.rem(t + tensors - k, tensors)
        to_peer(out.at[s], inn.at[s], send.at[s], recv.at[s], s).wait_recv()
        total[...] += inn[s].astype(jnp.float32)
        return 0

    lax.fori_loop(1, tensors, collect, 0)

    def finish(k, _):
        s = lax.rem(t + k, tensors)
        to_peer(out.at[s], inn.at[t], send.at[s], recv.at[t], s).wait_send()
        pair(s).wait_send()
        return 0

    lax.fori_loop(1, tensors, finish, 0)
    pair(t).wait_send()


def gather_blocks(tensors, t, r, buf, sems, use):
    send, recv, pair_send, pair_recv = sems
    mine = 2 * t + r

    def spread(k, _):
        d = lax.rem(t + k, tensors)
        to_peer(buf.at[mine], buf.at[mine], send.at[d], recv.at[t], d).start()
        return 0

    lax.fori_loop(1, tensors, spread, 0)

    def pair(s, q):
        return to_sibling(buf.at[q], buf.at[q], pair_send.at[s], pair_recv.at[s], r)

    pair(t, mine).start()
    use(mine)

    def near(k, _):
        s = lax.rem(t + tensors - k, tensors)
        q = 2 * s + r
        to_peer(buf.at[q], buf.at[q], send.at[s], recv.at[s], s).wait_recv()
        pair(s, q).start()
        use(q)
        return 0

    lax.fori_loop(1, tensors, near, 0)

    def far(k, _):
        s = lax.rem(t + tensors - k, tensors)
        q = 2 * s + 1 - r
        pair(s, q).wait_recv()
        use(q)
        return 0

    lax.fori_loop(0, tensors, far, 0)

    def finish(k, _):
        s = lax.rem(t + k, tensors)
        to_peer(buf.at[mine], buf.at[mine], send.at[s], recv.at[t], s).wait_send()
        pair(s, 2 * s + r).wait_send()
        return 0

    lax.fori_loop(1, tensors, finish, 0)
    pair(t, mine).wait_send()


def front_kernel(
    tensors, context, w_out, residual, fc_rest, w_fc, captured, features,
    pair_out, pair_in, out, inn, total, cap_buf, feat_buf, *sems,
):
    t, r = lax.axis_index("tensor"), lax.axis_index("role")
    cols = w_fc.shape[1]
    mine = 2 * t + r
    greet(tensors, t, r)

    def part(q):
        return product(context[...], w_out[:, pl.ds(pl.multiple_of(q * cols, cols), cols)])

    scatter_sum(
        tensors, t, r, part, lambda x: x.astype(jnp.bfloat16),
        (pair_out, pair_in, out, inn), sems[:4], total,
    )
    cap_buf[mine] = (total[...] + residual[...].astype(jnp.float32)).astype(jnp.bfloat16)
    total[...] = fc_rest[...].astype(jnp.float32)

    def multiply(q):
        block = cap_buf[q]
        captured[q] = block
        total[...] += product(block, w_fc[pl.ds(pl.multiple_of(q * cols, cols), cols), :])

    gather_blocks(tensors, t, r, cap_buf, sems[4:8], multiply)
    feat_buf[mine] = total[...].astype(jnp.bfloat16)

    def place(q):
        features[:, pl.ds(pl.multiple_of(q * cols, cols), cols)] = feat_buf[q]

    gather_blocks(tensors, t, r, feat_buf, sems[8:12], place)


def front(tensors, context, w_out, residual, fc_rest, w_fc):
    rows = context.shape[0]
    width, cols = w_fc.shape
    blocks = 2 * tensors
    return pl.pallas_call(
        functools.partial(front_kernel, tensors),
        out_shape=(
            jax.ShapeDtypeStruct((blocks, rows, cols), jnp.bfloat16),
            jax.ShapeDtypeStruct((rows, width), jnp.bfloat16),
        ),
        in_specs=[in_vmem()] * 5,
        out_specs=(in_vmem(), in_vmem()),
        scratch_shapes=[
            pltpu.VMEM((tensors, rows, cols), jnp.float32),
            pltpu.VMEM((tensors, rows, cols), jnp.float32),
            pltpu.VMEM((tensors, rows, cols), jnp.bfloat16),
            pltpu.VMEM((tensors, rows, cols), jnp.bfloat16),
            pltpu.VMEM((rows, cols), jnp.float32),
            pltpu.VMEM((blocks, rows, cols), jnp.bfloat16),
            pltpu.VMEM((blocks, rows, cols), jnp.bfloat16),
        ]
        + [pltpu.SemaphoreType.DMA((tensors,))] * 12,
        compiler_params=pltpu.CompilerParams(
            collective_id=0, has_side_effects=True, vmem_limit_bytes=VMEM_BYTES
        ),
    )(context, w_out, residual, fc_rest, w_fc)


def stats_kernel(tensors, stats, summed, buf, send, recv):
    t, r = lax.axis_index("tensor"), lax.axis_index("role")
    blocks = 2 * tensors
    mine = 2 * t + r
    barrier = pltpu.get_barrier_semaphore()

    def where(k):
        q = lax.rem(mine + k, blocks)
        return q, {"tensor": q // 2, "role": lax.rem(q, 2)}

    def hello(k, _):
        pl.semaphore_signal(barrier, inc=1, device_id=where(k)[1], device_id_type=MESH)
        return 0

    lax.fori_loop(1, blocks, hello, 0)
    pl.semaphore_wait(barrier, blocks - 1)

    def copy(q, slot, target):
        return pltpu.make_async_remote_copy(
            src_ref=stats, dst_ref=buf.at[slot], send_sem=send.at[q], recv_sem=recv.at[slot],
            device_id=target, device_id_type=MESH,
        )

    def spread(k, _):
        q, target = where(k)
        copy(q, mine, target).start()
        return 0

    lax.fori_loop(1, blocks, spread, 0)
    buf[mine] = stats[...]

    def collect(k, _):
        q, target = where(k)
        copy(q, q, target).wait_recv()
        copy(q, mine, target).wait_send()
        return 0

    lax.fori_loop(1, blocks, collect, 0)
    summed[...] = jnp.sum(buf[...], axis=0)


def group_sum(tensors, stats):
    blocks = 2 * tensors
    return pl.pallas_call(
        functools.partial(stats_kernel, tensors),
        out_shape=jax.ShapeDtypeStruct(stats.shape, jnp.float32),
        in_specs=[in_vmem()],
        out_specs=in_vmem(),
        scratch_shapes=[
            pltpu.VMEM((blocks,) + stats.shape, jnp.float32),
            pltpu.SemaphoreType.DMA((blocks,)),
            pltpu.SemaphoreType.DMA((blocks,)),
        ],
        compiler_params=pltpu.CompilerParams(
            collective_id=1, has_side_effects=True, vmem_limit_bytes=VMEM_BYTES
        ),
    )(stats)


def back_kernel(
    tensors, dlogits, w_lm, scales, gain, features, summed, pair_out, pair_in, out, inn, *sems
):
    t, r = lax.axis_index("tensor"), lax.axis_index("role")
    rows, cols = features.shape[0], out.shape[2]
    greet(tensors, t, r)
    line = lax.broadcasted_iota(jnp.int32, (EXTRA, cols), 0)

    def part(q):
        span = pl.ds(pl.multiple_of(q * cols, cols), cols)
        grads = lax.dot_general(
            dlogits[...], w_lm[span, :], (((1,), (1,)), ((), ())), preferred_element_type=jnp.float32
        )
        one, two = grads[:rows], grads[rows:]
        level = gain[:, span]
        here = scales[:, 0:1] * one + scales[:, 1:2] * two
        later = scales[:, 2:3] * pltpu.roll(two, rows - 1, 0) * level
        gain_part = jnp.sum(
            features[:, span].astype(jnp.float32) * (here + 2.0 * later), axis=0, keepdims=True
        )
        return jnp.concatenate(
            [level * (here + later), jnp.where(line == 0, gain_part, 0.0)], axis=0
        )

    def narrow(x):
        gain_row = x[rows : rows + 1]
        high = gain_row.astype(jnp.bfloat16).astype(jnp.float32)
        tail = jnp.where(line == 0, high, jnp.where(line == 1, gain_row - high, 0.0))
        return jnp.concatenate([x[:rows], tail], axis=0).astype(jnp.bfloat16)

    scatter_sum(tensors, t, r, part, narrow, (pair_out, pair_in, out, inn), sems, summed)


def back(tensors, dlogits, w_lm, scales, gain, features):
    rows, width = features.shape
    cols = width // (2 * tensors)
    tall = rows + EXTRA
    return pl.pallas_call(
        functools.partial(back_kernel, tensors),
        out_shape=jax.ShapeDtypeStruct((tall, cols), jnp.float32),
        in_specs=[in_vmem()] * 5,
        out_specs=in_vmem(),
        scratch_shapes=[
            pltpu.VMEM((tensors, tall, cols), jnp.float32),
            pltpu.VMEM((tensors, tall, cols), jnp.float32),
            pltpu.VMEM((tensors, tall, cols), jnp.bfloat16),
            pltpu.VMEM((tensors, tall, cols), jnp.bfloat16),
        ]
        + [pltpu.SemaphoreType.DMA((tensors,))] * 4,
        compiler_params=pltpu.CompilerParams(
            collective_id=2, has_side_effects=True, vmem_limit_bytes=VMEM_BYTES
        ),
    )(dlogits, w_lm, scales, gain, features)


def later_row(x):
    return jnp.concatenate([x[1:], jnp.zeros_like(x[:1])], axis=0)


def earlier_row(x):
    return jnp.concatenate([jnp.zeros_like(x[:1]), x[:-1]], axis=0)


def on_device(
    context, w_out, residual, fc_rest, w_fc, norm_gain, w_lm, tokens, segments, vocab_map
):
    tensors = lax.axis_size("tensor")
    position = lax.axis_index(("tensor", "role"))
    rows = tokens.shape[0] - 2
    width, cols = w_fc.shape
    vocab_own = w_lm.shape[1]

    gain = lax.all_gather(norm_gain, ("tensor", "role"), axis=0, tiled=True)[None, :]
    seg_now = segments[:rows]
    follows = jnp.concatenate(
        [
            jnp.zeros((1,), jnp.float32),
            (segments[1:rows] == segments[: rows - 1]).astype(jnp.float32),
        ]
    )
    labels_all = vocab_map[tokens]
    columns = position * vocab_own + jnp.arange(vocab_own, dtype=jnp.int32)

    captured, features = front(tensors, context, w_out, residual, fc_rest, w_fc)

    state = features.astype(jnp.float32)
    scale_one = lax.rsqrt(jnp.sum(state * state, axis=1) / width + EPS)
    normed_one = (state * scale_one[:, None] * gain).astype(jnp.bfloat16)
    shifted = earlier_row(normed_one).astype(jnp.float32) * follows[:, None]
    second = state + shifted
    scale_two = lax.rsqrt(jnp.sum(second * second, axis=1) / width + EPS)
    normed_two = (second * scale_two[:, None] * gain).astype(jnp.bfloat16)
    cross = jnp.sum(shifted * second, axis=1) / width

    logits = product(jnp.concatenate([normed_one, normed_two], axis=0), w_lm)
    logits_one, logits_two = logits[:rows], logits[rows:]

    def label_set(shift):
        labels = labels_all[shift : shift + rows]
        usable = ((labels >= 0) & (segments[shift : shift + rows] == seg_now)).astype(jnp.float32)
        return columns[None, :] == labels[:, None], usable

    matches_one, usable_one = label_set(1)
    matches_two, usable_two = label_set(2)
    powers_one, powers_two = jnp.exp(logits_one), jnp.exp(logits_two)

    def over(values):
        return jnp.sum(values, axis=1)

    stats = jnp.stack(
        [
            over(powers_one),
            over(powers_two),
            over(powers_one * (logits_one * SHRINK)),
            over(powers_two * (logits_two * SHRINK)),
            over(powers_two * (logits_one * SHRINK)),
            over(jnp.where(matches_one, logits_one, 0.0)),
            over(jnp.where(matches_two, logits_two, 0.0)),
            over(jnp.where(matches_two, logits_one, 0.0)),
        ]
    )
    (totals_one, totals_two, mean_one, mean_two, mean_mixed, picked_one, picked_two, picked_mixed) = (
        group_sum(tensors, stats)
    )

    def average(totals, picked, usable):
        return jnp.sum(usable * (jnp.log(totals) - picked)) / jnp.maximum(jnp.sum(usable), 1.0)

    losses = jnp.stack(
        [average(totals_one, picked_one, usable_one), average(totals_two, picked_two, usable_two)]
    )

    def gradient(powers, totals, matches, weight):
        return (
            weight[:, None] * (powers / totals[:, None] - matches.astype(jnp.float32))
        ).astype(jnp.bfloat16)

    weight_one, weight_two = usable_one, 0.8 * usable_two
    dlogits = jnp.concatenate(
        [
            gradient(powers_one, totals_one, matches_one, weight_one),
            gradient(powers_two, totals_two, matches_two, weight_two),
        ],
        axis=0,
    )
    follows_next = later_row(follows)
    link = scale_one * follows_next * later_row(scale_two)
    scales = jnp.stack([scale_one, scale_two, link], axis=1)
    summed = back(tensors, dlogits, w_lm, scales, gain, features)

    dot_one = weight_one * (mean_one / (SHRINK * totals_one) - picked_one)
    dot_two = weight_two * (mean_two / (SHRINK * totals_two) - picked_two)
    dot_mixed = weight_two * (mean_mixed / (SHRINK * totals_two) - picked_mixed)
    projection_two = dot_two / (scale_two * width)
    pull_two = scale_two**3 * projection_two
    back_link = follows * (dot_two / scale_two - dot_mixed / scale_one) / width
    through = later_row(follows * (scale_two * back_link - pull_two * cross))
    projection_one = (dot_one / width + through) / scale_one
    pull_one = scale_one**3 * projection_one

    own = position * cols
    state_own = lax.dynamic_slice_in_dim(features, own, cols, axis=1).astype(jnp.float32)
    normed_own = lax.dynamic_slice_in_dim(normed_one, own, cols, axis=1).astype(jnp.float32)
    second_own = state_own + earlier_row(normed_own) * follows[:, None]
    pulled = later_row(second_own * (follows * pull_two)[:, None]) * scale_one[:, None]
    gradient_sum = (
        summed[:rows]
        - norm_gain[None, :] * pulled
        - state_own * pull_one[:, None]
        - second_own * pull_two[:, None]
    ).astype(jnp.bfloat16)
    grad_gain = summed[rows] + summed[rows + 1] - jnp.sum(pulled * state_own, axis=0)
    grad_fc = (
        jnp.einsum("pti,tj->pij", captured, gradient_sum, preferred_element_type=jnp.float32)
        .astype(jnp.bfloat16)
        .reshape(width, cols)
    )
    return (losses, grad_fc, grad_gain)


def solution(mesh):
    placed = (
        P("groups", ("tensor", "role")),
        P(("tensor", "role"), None),
        P("groups", ("tensor", "role")),
        P("groups", ("tensor", "role")),
        P(None, ("tensor", "role")),
        P(("tensor", "role")),
        P(None, ("tensor", "role")),
        P("groups"),
        P("groups"),
        P("groups"),
    )
    return jax.shard_map(
        on_device,
        mesh=mesh,
        in_specs=placed,
        out_specs=(P("groups"), P("groups", ("tensor", "role")), P(("groups", "tensor", "role"))),
        check_vma=False,
    )
```

```python
import functools

import jax
import jax.numpy as jnp
from jax import lax
from jax.experimental import pallas as pl
from jax.experimental.pallas import tpu as pltpu
from jax.sharding import PartitionSpec as P

EPS = 1e-05
SHRINK = 1.0 / 1024.0
VMEM_BYTES = 56 * 1024 * 1024
EXTRA = 16
MESH = pl.DeviceIdType.MESH


def in_vmem():
    return pl.BlockSpec(memory_space=pltpu.VMEM)


def product(a, b):
    return jnp.dot(a, b, preferred_element_type=jnp.float32)


class Place:
    def __init__(self, tensors):
        self.lanes = 2 if tensors == 8 else 1
        self.depth = tensors // self.lanes
        self.tensors = tensors
        self.t, self.r = lax.axis_index("tensor"), lax.axis_index("role")
        self.z, self.y = self.t // self.lanes, lax.rem(self.t, self.lanes)
        self.mine = 2 * self.t + self.r

    def before(self, k):
        return lax.rem(self.z + self.depth - k, self.depth)

    def after(self, k):
        return lax.rem(self.z + k, self.depth)

    def across(self, z):
        return z * 2 + 1 - self.y

    def along(self, z):
        return z * self.lanes + self.y

    def neighbours(self):
        others = [{"role": 1 - self.r}]
        if self.lanes == 2:
            others.append({"tensor": self.across(self.z)})
        return others

    def greet(self):
        barrier = pltpu.get_barrier_semaphore()

        def hello(k, _):
            pl.semaphore_signal(
                barrier, inc=1, device_id={"tensor": self.along(self.after(k))}, device_id_type=MESH
            )
            return 0

        lax.fori_loop(1, self.depth, hello, 0)
        for other in self.neighbours():
            pl.semaphore_signal(barrier, inc=1, device_id=other, device_id_type=MESH)
        pl.semaphore_wait(barrier, self.depth - 1 + len(self.neighbours()))


def remote(src, dst, send_sem, recv_sem, target):
    return pltpu.make_async_remote_copy(
        src_ref=src, dst_ref=dst, send_sem=send_sem, recv_sem=recv_sem,
        device_id=target, device_id_type=MESH,
    )


def scatter_scratch(tensors, rows, cols):
    depth = tensors // (2 if tensors == 8 else 1)
    return [
        pltpu.VMEM((tensors, rows, cols), jnp.float32),
        pltpu.VMEM((tensors, rows, cols), jnp.float32),
        pltpu.VMEM((depth, rows, cols), jnp.bfloat16),
        pltpu.VMEM((depth, rows, cols), jnp.bfloat16),
        pltpu.VMEM((depth, rows, cols), jnp.bfloat16),
        pltpu.VMEM((depth, rows, cols), jnp.bfloat16),
    ] + [pltpu.SemaphoreType.DMA((tensors,))] * 2 + [pltpu.SemaphoreType.DMA((depth,))] * 4


def gather_sems(tensors):
    return [pltpu.SemaphoreType.DMA((tensors,))] * 6


def scatter_sum(at, part, narrow, widen, scratch, total):
    pair_out, pair_in, y_out, y_in, z_out, z_in = scratch[:6]
    pair_send, pair_recv, y_send, y_recv, z_send, z_recv = scratch[6:]
    depth, r = at.depth, at.r

    def pair(d):
        return remote(
            pair_out.at[d], pair_in.at[d], pair_send.at[d], pair_recv.at[d], {"role": 1 - r}
        )

    def cross(z):
        return remote(
            y_out.at[z], y_in.at[z], y_send.at[z], y_recv.at[z], {"tensor": at.across(at.z)}
        )

    def line(z):
        return remote(
            z_out.at[z], z_in.at[at.z], z_send.at[z], z_recv.at[at.z], {"tensor": at.along(z)}
        )

    def arrived(z):
        return remote(
            z_out.at[z], z_in.at[z], z_send.at[z], z_recv.at[z], {"tensor": at.along(z)}
        )

    def dests(z):
        return [at.across(z), at.along(z)] if at.lanes == 2 else [at.along(z)]

    def first(k):
        for d in dests(at.after(k)):
            pair_out[d] = part(2 * d + 1 - r)
            pair(d).start()

    def second(k):
        z = at.after(k)
        if at.lanes == 2:
            d = at.across(z)
            own = part(2 * d + r)
            pair(d).wait_recv()
            y_out[z] = narrow(own + pair_in[d])
            cross(z).start()
        d = at.along(z)
        own = part(2 * d + r)
        pair(d).wait_recv()
        pair_in[d] = own + pair_in[d]

    def merged(z):
        value = pair_in[at.along(z)]
        if at.lanes == 2:
            cross(z).wait_recv()
            value = value + widen(y_in[z])
        return value

    def third(k):
        z = at.after(k)
        z_out[z] = narrow(merged(z))
        line(z).start()

    first(1)
    if depth > 2:
        first(2)
    second(1)

    def step(k, _):
        first(k + 1)
        second(k)
        third(k - 1)
        return 0

    lax.fori_loop(2, depth, step, 0)
    if depth == 2:
        first(depth)
    second(depth)
    third(depth - 1)
    total[...] = merged(at.z)

    def collect(k, _):
        z = at.before(k)
        arrived(z).wait_recv()
        total[...] += widen(z_in[z])
        return 0

    lax.fori_loop(1, depth, collect, 0)

    def finish(k, _):
        z = at.after(k)
        line(z).wait_send()
        return 0

    lax.fori_loop(1, depth, finish, 0)

    def finish_near(k, _):
        z = at.after(k)
        for d in dests(z):
            pair(d).wait_send()
        if at.lanes == 2:
            cross(z).wait_send()
        return 0

    lax.fori_loop(0, depth, finish_near, 0)


class Gather:
    def __init__(self, at, buf, sems, use):
        self.at, self.buf, self.sems, self.use = at, buf, sems, use

    def line(self, z):
        at, mine = self.at, self.buf.at[self.at.mine]
        return remote(
            mine, mine, self.sems[0].at[z], self.sems[1].at[at.z], {"tensor": at.along(z)}
        )

    def arrived(self, z):
        at = self.at
        block = self.buf.at[2 * at.along(z) + at.r]
        return remote(
            block, block, self.sems[0].at[z], self.sems[1].at[z], {"tensor": at.along(z)}
        )

    def cross(self, z, t):
        at = self.at
        block = self.buf.at[2 * t + at.r]
        return remote(
            block, block, self.sems[2].at[z], self.sems[3].at[z], {"tensor": at.across(at.z)}
        )

    def pair(self, t, r):
        block = self.buf.at[2 * t + r]
        return remote(
            block, block, self.sems[4].at[t], self.sems[5].at[t], {"role": 1 - self.at.r}
        )

    def start(self):
        at = self.at
        if at.lanes == 2:
            self.cross(at.z, at.t).start()

        def spread(k, _):
            self.line(at.after(k)).start()
            return 0

        lax.fori_loop(1, at.depth, spread, 0)
        self.pair(at.t, at.r).start()

    def over(self, k):
        at = self.at
        if at.lanes == 2:
            z = at.before(k)
            t = at.across(z)
            self.cross(z, t).wait_recv()
            self.pair(t, at.r).start()
            self.use(2 * t + at.r)

    def relay(self):
        at = self.at
        self.use(at.mine)

        def step(k, _):
            z = at.before(k)
            t = at.along(z)
            self.arrived(z).wait_recv()
            if at.lanes == 2:
                self.cross(z, t).start()
            self.pair(t, at.r).start()
            self.use(2 * t + at.r)
            self.over(k - 1)
            return 0

        lax.fori_loop(1, at.depth, step, 0)
        self.over(at.depth - 1)

    def finish(self):
        at = self.at

        def far(k, _):
            z = at.before(k)
            for t in [at.along(z)] + ([at.across(z)] if at.lanes == 2 else []):
                self.pair(t, 1 - at.r).wait_recv()
                self.use(2 * t + 1 - at.r)
            return 0

        lax.fori_loop(0, at.depth, far, 0)

        def sent(k, _):
            z = at.after(k)
            self.pair(at.along(z), at.r).wait_send()
            if at.lanes == 2:
                self.cross(z, at.along(z)).wait_send()
                self.pair(at.across(z), at.r).wait_send()
            return 0

        lax.fori_loop(0, at.depth, sent, 0)

        def line_sent(k, _):
            self.line(at.after(k)).wait_send()
            return 0

        lax.fori_loop(1, at.depth, line_sent, 0)


def front_kernel(
    tensors, context, w_out, residual, fc_rest, w_fc, own_gain, captured, features, gain,
    total, cap_buf, feat_buf, gain_buf, *scratch,
):
    at = Place(tensors)
    cols = w_fc.shape[1]
    gain_buf[at.mine] = jnp.broadcast_to(own_gain[...], gain_buf.shape[1:])
    at.greet()

    def span(q):
        return pl.ds(pl.multiple_of(q * cols, cols), cols)

    def keep_gain(q):
        gain[:, span(q)] = gain_buf[q][:1]

    def multiply(q):
        block = cap_buf[q]
        captured[q] = block
        total[...] += product(block, w_fc[span(q), :])

    def place(q):
        features[:, span(q)] = feat_buf[q]

    gains = Gather(at, gain_buf, scratch[12:18], keep_gain)
    caps = Gather(at, cap_buf, scratch[18:24], multiply)
    feats = Gather(at, feat_buf, scratch[24:30], place)

    gains.start()
    scatter_sum(
        at, lambda q: product(context[...], w_out[:, span(q)]), lambda x: x.astype(jnp.bfloat16),
        lambda x: x.astype(jnp.float32), scratch[:12], total,
    )
    cap_buf[at.mine] = (total[...] + residual[...].astype(jnp.float32)).astype(jnp.bfloat16)
    caps.start()
    total[...] = fc_rest[...].astype(jnp.float32)
    gains.relay()
    caps.relay()
    caps.finish()
    feat_buf[at.mine] = total[...].astype(jnp.bfloat16)
    feats.start()
    gains.finish()
    feats.relay()
    feats.finish()


def front(tensors, context, w_out, residual, fc_rest, w_fc, norm_gain):
    rows = context.shape[0]
    width, cols = w_fc.shape
    blocks = 2 * tensors
    return pl.pallas_call(
        functools.partial(front_kernel, tensors),
        out_shape=(
            jax.ShapeDtypeStruct((blocks, rows, cols), jnp.bfloat16),
            jax.ShapeDtypeStruct((rows, width), jnp.bfloat16),
            jax.ShapeDtypeStruct((1, width), jnp.float32),
        ),
        in_specs=[in_vmem()] * 6,
        out_specs=(in_vmem(), in_vmem(), in_vmem()),
        scratch_shapes=[
            pltpu.VMEM((rows, cols), jnp.float32),
            pltpu.VMEM((blocks, rows, cols), jnp.bfloat16),
            pltpu.VMEM((blocks, rows, cols), jnp.bfloat16),
            pltpu.VMEM((blocks, 8, cols), jnp.float32),
        ]
        + scatter_scratch(tensors, rows, cols)
        + gather_sems(tensors) * 3,
        compiler_params=pltpu.CompilerParams(
            collective_id=0, has_side_effects=True, vmem_limit_bytes=VMEM_BYTES
        ),
    )(context, w_out, residual, fc_rest, w_fc, norm_gain[None, :])


def stats_kernel(tensors, stats, summed, buf, send, recv):
    t, r = lax.axis_index("tensor"), lax.axis_index("role")
    blocks = 2 * tensors
    mine = 2 * t + r
    barrier = pltpu.get_barrier_semaphore()

    def where(k):
        q = lax.rem(mine + k, blocks)
        return q, {"tensor": q // 2, "role": lax.rem(q, 2)}

    def hello(k, _):
        pl.semaphore_signal(barrier, inc=1, device_id=where(k)[1], device_id_type=MESH)
        return 0

    lax.fori_loop(1, blocks, hello, 0)
    pl.semaphore_wait(barrier, blocks - 1)

    def copy(q, slot, target):
        return pltpu.make_async_remote_copy(
            src_ref=stats, dst_ref=buf.at[slot], send_sem=send.at[q], recv_sem=recv.at[slot],
            device_id=target, device_id_type=MESH,
        )

    def spread(k, _):
        q, target = where(k)
        copy(q, mine, target).start()
        return 0

    lax.fori_loop(1, blocks, spread, 0)
    buf[mine] = stats[...]

    def collect(k, _):
        q, target = where(k)
        copy(q, q, target).wait_recv()
        copy(q, mine, target).wait_send()
        return 0

    lax.fori_loop(1, blocks, collect, 0)
    summed[...] = jnp.sum(buf[...], axis=0)


def group_sum(tensors, stats):
    blocks = 2 * tensors
    return pl.pallas_call(
        functools.partial(stats_kernel, tensors),
        out_shape=jax.ShapeDtypeStruct(stats.shape, jnp.float32),
        in_specs=[in_vmem()],
        out_specs=in_vmem(),
        scratch_shapes=[
            pltpu.VMEM((blocks,) + stats.shape, jnp.float32),
            pltpu.SemaphoreType.DMA((blocks,)),
            pltpu.SemaphoreType.DMA((blocks,)),
        ],
        compiler_params=pltpu.CompilerParams(
            collective_id=1, has_side_effects=True, vmem_limit_bytes=VMEM_BYTES
        ),
    )(stats)


def back_kernel(tensors, dlogits, w_lm, scales, gain, features, summed, *scratch):
    at = Place(tensors)
    rows, cols = features.shape[0], summed.shape[1]
    at.greet()
    line = lax.broadcasted_iota(jnp.int32, (EXTRA, cols), 0)

    def part(q):
        span = pl.ds(pl.multiple_of(q * cols, cols), cols)
        grads = product(dlogits[...], w_lm[:, span])
        one, two = grads[:rows], grads[rows:]
        level = gain[:, span]
        here = scales[:, 0:1] * one + scales[:, 1:2] * two
        later = scales[:, 2:3] * pltpu.roll(two, rows - 1, 0) * level
        gain_part = jnp.sum(
            features[:, span].astype(jnp.float32) * (here + 2.0 * later), axis=0, keepdims=True
        )
        return jnp.concatenate(
            [level * (here + later), jnp.where(line == 0, gain_part, 0.0)], axis=0
        )

    def narrow(x):
        gain_row = x[rows : rows + 1]
        high = gain_row.astype(jnp.bfloat16).astype(jnp.float32)
        tail = jnp.where(line == 0, high, jnp.where(line == 1, gain_row - high, 0.0))
        return jnp.concatenate([x[:rows], tail], axis=0).astype(jnp.bfloat16)

    def widen(x):
        wide = x.astype(jnp.float32)
        gain_row = wide[rows : rows + 1] + wide[rows + 1 : rows + 2]
        return jnp.concatenate([wide[:rows], jnp.where(line == 0, gain_row, 0.0)], axis=0)

    scatter_sum(at, part, narrow, widen, scratch, summed)


def back(tensors, dlogits, w_lm, scales, gain, features):
    rows, width = features.shape
    cols = width // (2 * tensors)
    tall = rows + EXTRA
    return pl.pallas_call(
        functools.partial(back_kernel, tensors),
        out_shape=jax.ShapeDtypeStruct((tall, cols), jnp.float32),
        in_specs=[in_vmem()] * 5,
        out_specs=in_vmem(),
        scratch_shapes=scatter_scratch(tensors, tall, cols),
        compiler_params=pltpu.CompilerParams(
            collective_id=2, has_side_effects=True, vmem_limit_bytes=VMEM_BYTES
        ),
    )(dlogits, w_lm.T, scales, gain, features)


def later_row(x):
    return jnp.concatenate([x[1:], jnp.zeros_like(x[:1])], axis=0)


def earlier_row(x):
    return jnp.concatenate([jnp.zeros_like(x[:1]), x[:-1]], axis=0)


def on_device(
    context, w_out, residual, fc_rest, w_fc, norm_gain, w_lm, tokens, segments, vocab_map
):
    tensors = lax.axis_size("tensor")
    position = lax.axis_index(("tensor", "role"))
    rows = tokens.shape[0] - 2
    width, cols = w_fc.shape
    vocab_own = w_lm.shape[1]

    seg_now = segments[:rows]
    follows = jnp.concatenate(
        [
            jnp.zeros((1,), jnp.float32),
            (segments[1:rows] == segments[: rows - 1]).astype(jnp.float32),
        ]
    )
    labels_all = vocab_map[tokens]
    columns = position * vocab_own + jnp.arange(vocab_own, dtype=jnp.int32)

    captured, features, gain = front(tensors, context, w_out, residual, fc_rest, w_fc, norm_gain)

    state = features.astype(jnp.float32)
    scale_one = lax.rsqrt(jnp.sum(state * state, axis=1) / width + EPS)
    normed_one = (state * scale_one[:, None] * gain).astype(jnp.bfloat16)
    shifted = earlier_row(normed_one).astype(jnp.float32) * follows[:, None]
    second = state + shifted
    scale_two = lax.rsqrt(jnp.sum(second * second, axis=1) / width + EPS)
    normed_two = (second * scale_two[:, None] * gain).astype(jnp.bfloat16)
    cross = jnp.sum(shifted * second, axis=1) / width

    logits = product(jnp.concatenate([normed_one, normed_two], axis=0), w_lm)
    logits_one, logits_two = logits[:rows], logits[rows:]

    def label_set(shift):
        labels = labels_all[shift : shift + rows]
        usable = ((labels >= 0) & (segments[shift : shift + rows] == seg_now)).astype(jnp.float32)
        return columns[None, :] == labels[:, None], usable

    matches_one, usable_one = label_set(1)
    matches_two, usable_two = label_set(2)
    powers_one, powers_two = jnp.exp(logits_one), jnp.exp(logits_two)

    def over(values):
        return jnp.sum(values, axis=1)

    stats = jnp.stack(
        [
            over(powers_one),
            over(powers_two),
            over(powers_one * (logits_one * SHRINK)),
            over(powers_two * (logits_two * SHRINK)),
            over(powers_two * (logits_one * SHRINK)),
            over(jnp.where(matches_one, logits_one, 0.0)),
            over(jnp.where(matches_two, logits_two, 0.0)),
            over(jnp.where(matches_two, logits_one, 0.0)),
        ]
    )
    (totals_one, totals_two, mean_one, mean_two, mean_mixed, picked_one, picked_two, picked_mixed) = (
        group_sum(tensors, stats)
    )

    def average(totals, picked, usable):
        return jnp.sum(usable * (jnp.log(totals) - picked)) / jnp.maximum(jnp.sum(usable), 1.0)

    losses = jnp.stack(
        [average(totals_one, picked_one, usable_one), average(totals_two, picked_two, usable_two)]
    )

    def gradient(powers, totals, matches, weight):
        return (
            weight[:, None] * (powers / totals[:, None] - matches.astype(jnp.float32))
        ).astype(jnp.bfloat16)

    weight_one, weight_two = usable_one, 0.8 * usable_two
    dlogits = jnp.concatenate(
        [
            gradient(powers_one, totals_one, matches_one, weight_one),
            gradient(powers_two, totals_two, matches_two, weight_two),
        ],
        axis=0,
    )
    follows_next = later_row(follows)
    link = scale_one * follows_next * later_row(scale_two)
    scales = jnp.stack([scale_one, scale_two, link], axis=1)
    summed = back(tensors, dlogits, w_lm, scales, gain, features)

    dot_one = weight_one * (mean_one / (SHRINK * totals_one) - picked_one)
    dot_two = weight_two * (mean_two / (SHRINK * totals_two) - picked_two)
    dot_mixed = weight_two * (mean_mixed / (SHRINK * totals_two) - picked_mixed)
    projection_two = dot_two / (scale_two * width)
    pull_two = scale_two**3 * projection_two
    back_link = follows * (dot_two / scale_two - dot_mixed / scale_one) / width
    through = later_row(follows * (scale_two * back_link - pull_two * cross))
    projection_one = (dot_one / width + through) / scale_one
    pull_one = scale_one**3 * projection_one

    own = position * cols
    state_own = lax.dynamic_slice_in_dim(features, own, cols, axis=1).astype(jnp.float32)
    normed_own = lax.dynamic_slice_in_dim(normed_one, own, cols, axis=1).astype(jnp.float32)
    second_own = state_own + earlier_row(normed_own) * follows[:, None]
    pulled = later_row(second_own * (follows * pull_two)[:, None]) * scale_one[:, None]
    gradient_sum = (
        summed[:rows]
        - norm_gain[None, :] * pulled
        - state_own * pull_one[:, None]
        - second_own * pull_two[:, None]
    ).astype(jnp.bfloat16)
    grad_gain = summed[rows] - jnp.sum(pulled * state_own, axis=0)
    grad_fc = (
        jnp.einsum("pti,tj->pij", captured, gradient_sum, preferred_element_type=jnp.float32)
        .astype(jnp.bfloat16)
        .reshape(width, cols)
    )
    return (losses, grad_fc, grad_gain)


def solution(mesh):
    placed = (
        P("groups", ("tensor", "role")),
        P(("tensor", "role"), None),
        P("groups", ("tensor", "role")),
        P("groups", ("tensor", "role")),
        P(None, ("tensor", "role")),
        P(("tensor", "role")),
        P(None, ("tensor", "role")),
        P("groups"),
        P("groups"),
        P("groups"),
    )
    return jax.shard_map(
        on_device,
        mesh=mesh,
        in_specs=placed,
        out_specs=(P("groups"), P("groups", ("tensor", "role")), P(("groups", "tensor", "role"))),
        check_vma=False,
    )
```

```python
import functools

import jax
import jax.numpy as jnp
from jax import lax
from jax.experimental import pallas as pl
from jax.experimental.pallas import tpu as pltpu
from jax.sharding import PartitionSpec as P

EPS = 1e-05
SHRINK = 1.0 / 1024.0
VMEM_BYTES = 60 * 1024 * 1024
EXTRA = 16
LANES = 128
MESH = pl.DeviceIdType.MESH


def in_vmem():
    return pl.BlockSpec(memory_space=pltpu.VMEM)


def product(a, b):
    return jnp.dot(a, b, preferred_element_type=jnp.float32)


class Place:
    def __init__(self, tensors):
        self.lanes = 2 if tensors == 8 else 1
        self.depth = tensors // self.lanes
        self.tensors = tensors
        self.t, self.r = lax.axis_index("tensor"), lax.axis_index("role")
        self.z, self.y = self.t // self.lanes, lax.rem(self.t, self.lanes)
        self.mine = 2 * self.t + self.r

    def before(self, k):
        return lax.rem(self.z + self.depth - k, self.depth)

    def after(self, k):
        return lax.rem(self.z + k, self.depth)

    def across(self, z):
        return z * 2 + 1 - self.y

    def along(self, z):
        return z * self.lanes + self.y

    def other(self, k):
        q = lax.rem(self.mine + k, 2 * self.tensors)
        return q, {"tensor": q // 2, "role": lax.rem(q, 2)}

    def greet(self):
        barrier = pltpu.get_barrier_semaphore()
        others = 2 * self.tensors

        def hello(k, _):
            pl.semaphore_signal(barrier, inc=1, device_id=self.other(k)[1], device_id_type=MESH)
            return 0

        lax.fori_loop(1, others, hello, 0)
        pl.semaphore_wait(barrier, others - 1)


def remote(src, dst, send_sem, recv_sem, target):
    return pltpu.make_async_remote_copy(
        src_ref=src, dst_ref=dst, send_sem=send_sem, recv_sem=recv_sem,
        device_id=target, device_id_type=MESH,
    )


def scatter_scratch(tensors, rows, cols):
    depth = tensors // (2 if tensors == 8 else 1)
    return [pltpu.VMEM((tensors, rows, cols), jnp.float32)] * 2 + [
        pltpu.VMEM((depth, rows, cols), jnp.bfloat16)
    ] * 4


def scatter_sems(tensors):
    depth = tensors // (2 if tensors == 8 else 1)
    return [pltpu.SemaphoreType.DMA((tensors,))] * 2 + [pltpu.SemaphoreType.DMA((depth,))] * 4


def gather_sems(tensors):
    return [pltpu.SemaphoreType.DMA((tensors,))] * 6


def scatter_sum(at, part, narrow, widen, buffers, sems, total):
    height = total.shape[0]
    pair_out, pair_in, y_out, y_in, z_out, z_in = [b.at[:, pl.ds(0, height), :] for b in buffers]
    pair_send, pair_recv, y_send, y_recv, z_send, z_recv = sems
    depth, r = at.depth, at.r

    def pair(d):
        return remote(
            pair_out.at[d], pair_in.at[d], pair_send.at[d], pair_recv.at[d], {"role": 1 - r}
        )

    def cross(z):
        return remote(
            y_out.at[z], y_in.at[z], y_send.at[z], y_recv.at[z], {"tensor": at.across(at.z)}
        )

    def line(z):
        return remote(
            z_out.at[z], z_in.at[at.z], z_send.at[z], z_recv.at[at.z], {"tensor": at.along(z)}
        )

    def arrived(z):
        return remote(
            z_out.at[z], z_in.at[z], z_send.at[z], z_recv.at[z], {"tensor": at.along(z)}
        )

    def dests(z):
        return [at.across(z), at.along(z)] if at.lanes == 2 else [at.along(z)]

    def first(k):
        for d in dests(at.after(k)):
            pair_out[d] = part(2 * d + 1 - r)
            pair(d).start()

    def second(k):
        z = at.after(k)
        if at.lanes == 2:
            d = at.across(z)
            own = part(2 * d + r)
            pair(d).wait_recv()
            y_out[z] = narrow(own + pair_in[d])
            cross(z).start()
        d = at.along(z)
        own = part(2 * d + r)
        pair(d).wait_recv()
        pair_in[d] = own + pair_in[d]

    def merged(z):
        value = pair_in[at.along(z)]
        if at.lanes == 2:
            cross(z).wait_recv()
            value = value + widen(y_in[z])
        return value

    def third(k):
        z = at.after(k)
        z_out[z] = narrow(merged(z))
        line(z).start()

    first(1)
    if depth > 2:
        first(2)
    second(1)

    def step(k, _):
        first(k + 1)
        second(k)
        third(k - 1)
        return 0

    lax.fori_loop(2, depth, step, 0)
    if depth == 2:
        first(depth)
    second(depth)
    third(depth - 1)
    total[...] = merged(at.z)

    def collect(k, _):
        z = at.before(k)
        arrived(z).wait_recv()
        total[...] += widen(z_in[z])
        return 0

    lax.fori_loop(1, depth, collect, 0)

    def finish(k, _):
        z = at.after(k)
        line(z).wait_send()
        return 0

    lax.fori_loop(1, depth, finish, 0)

    def finish_near(k, _):
        z = at.after(k)
        for d in dests(z):
            pair(d).wait_send()
        if at.lanes == 2:
            cross(z).wait_send()
        return 0

    lax.fori_loop(0, depth, finish_near, 0)


class Gather:
    def __init__(self, at, buf, sems, use):
        self.at, self.buf, self.sems, self.use = at, buf, sems, use

    def line(self, z):
        at, mine = self.at, self.buf.at[self.at.mine]
        return remote(
            mine, mine, self.sems[0].at[z], self.sems[1].at[at.z], {"tensor": at.along(z)}
        )

    def arrived(self, z):
        at = self.at
        block = self.buf.at[2 * at.along(z) + at.r]
        return remote(
            block, block, self.sems[0].at[z], self.sems[1].at[z], {"tensor": at.along(z)}
        )

    def cross(self, z, t):
        at = self.at
        block = self.buf.at[2 * t + at.r]
        return remote(
            block, block, self.sems[2].at[z], self.sems[3].at[z], {"tensor": at.across(at.z)}
        )

    def pair(self, t, r):
        block = self.buf.at[2 * t + r]
        return remote(
            block, block, self.sems[4].at[t], self.sems[5].at[t], {"role": 1 - self.at.r}
        )

    def start(self):
        at = self.at
        if at.lanes == 2:
            self.cross(at.z, at.t).start()

        def spread(k, _):
            self.line(at.after(k)).start()
            return 0

        lax.fori_loop(1, at.depth, spread, 0)
        self.pair(at.t, at.r).start()

    def over(self, k):
        at = self.at
        if at.lanes == 2:
            z = at.before(k)
            t = at.across(z)
            self.cross(z, t).wait_recv()
            self.pair(t, at.r).start()
            self.use(2 * t + at.r)

    def relay(self):
        at = self.at
        self.use(at.mine)

        def step(k, _):
            z = at.before(k)
            t = at.along(z)
            self.arrived(z).wait_recv()
            if at.lanes == 2:
                self.cross(z, t).start()
            self.pair(t, at.r).start()
            self.use(2 * t + at.r)
            self.over(k - 1)
            return 0

        lax.fori_loop(1, at.depth, step, 0)
        self.over(at.depth - 1)

    def finish(self):
        at = self.at

        def far(k, _):
            z = at.before(k)
            for t in [at.along(z)] + ([at.across(z)] if at.lanes == 2 else []):
                self.pair(t, 1 - at.r).wait_recv()
                self.use(2 * t + 1 - at.r)
            return 0

        lax.fori_loop(0, at.depth, far, 0)

        def sent(k, _):
            z = at.after(k)
            self.pair(at.along(z), at.r).wait_send()
            if at.lanes == 2:
                self.cross(z, at.along(z)).wait_send()
                self.pair(at.across(z), at.r).wait_send()
            return 0

        lax.fori_loop(0, at.depth, sent, 0)

        def line_sent(k, _):
            self.line(at.after(k)).wait_send()
            return 0

        lax.fori_loop(1, at.depth, line_sent, 0)


def fold(x):
    total = x[:, :LANES]
    for start in range(LANES, x.shape[1], LANES):
        total = total + x[:, start : start + LANES]
    return total


def spread_sum(x):
    return jnp.broadcast_to(jnp.sum(x, axis=1, keepdims=True), x.shape)


def earlier(x):
    return pltpu.roll(x, 1, 0)


def later(x):
    return pltpu.roll(x, x.shape[0] - 1, 0)


def narrow_plain(x):
    return x.astype(jnp.bfloat16)


def widen_plain(x):
    return x.astype(jnp.float32)


def step_kernel(
    tensors, context, w_out, residual, fc_rest, own_gain, marks, flags, w_fc_far, w_lm_far,
    captured, grad_state, grad_gain, losses,
    w_fc, w_lm, total, cap_buf, feat_buf, gain_buf, moments, logits, dlogits, stats, shared,
    summed, load, *scratch,
):
    at = Place(tensors)
    rows, cols = context.shape[0], w_fc.shape[1]
    width, vocab_own = w_fc.shape[0], w_lm.shape[0]
    blocks = 2 * tensors
    buffers, sems = scratch[:6], scratch[6:]
    load_fc = pltpu.make_async_copy(w_fc_far, w_fc, load.at[0])
    load_lm = pltpu.make_async_copy(w_lm_far, w_lm, load.at[1])
    load_fc.start()
    load_lm.start()
    gain_buf[at.mine] = jnp.broadcast_to(own_gain[...], gain_buf.shape[1:])
    at.greet()

    def span(q):
        return pl.ds(pl.multiple_of(q * cols, cols), cols)

    def level(q):
        return gain_buf[q][:1]

    def multiply(q):
        block = cap_buf[q]
        captured[q] = block
        total[...] += product(block, w_fc[span(q), :])

    def head(q):
        state = feat_buf[q].astype(jnp.float32)
        scaled = state * level(q)
        before = earlier(scaled)
        moments[0] += fold(state * state)
        moments[1] += fold(state * before)
        moments[2] += fold(before * before)
        both = jnp.concatenate([scaled, before * level(q)], axis=0).astype(jnp.bfloat16)
        logits[...] += lax.dot_general(
            both, w_lm[:, span(q)], (((1,), (1,)), ((), ())), preferred_element_type=jnp.float32
        )

    gains = Gather(at, gain_buf, sems[0:6], lambda q: None)
    caps = Gather(at, cap_buf, sems[6:12], multiply)
    feats = Gather(at, feat_buf, sems[12:18], head)

    gains.start()
    scatter_sum(
        at, lambda q: product(context[...], w_out[:, span(q)]), narrow_plain, widen_plain,
        buffers, sems[18:24], total,
    )
    cap_buf[at.mine] = (total[...] + residual[...].astype(jnp.float32)).astype(jnp.bfloat16)
    caps.start()
    total[...] = fc_rest[...].astype(jnp.float32)
    moments[...] = jnp.zeros_like(moments)
    logits[...] = jnp.zeros_like(logits)
    gains.relay()
    load_fc.wait()
    caps.relay()
    caps.finish()
    feat_buf[at.mine] = total[...].astype(jnp.bfloat16)
    feats.start()
    gains.finish()
    load_lm.wait()
    feats.relay()
    feats.finish()

    follows = jnp.broadcast_to(flags[:, 0:1], (rows, LANES))
    usable_one, usable_two = flags[:, 1:2], flags[:, 2:3]
    squares, mixed, squares_before = [spread_sum(moments[i]) / width for i in range(3)]
    scale_one = lax.rsqrt(squares + EPS)
    link = follows * earlier(scale_one)
    cross = link * (mixed + link * squares_before)
    scale_two = lax.rsqrt(jnp.maximum(squares + link * mixed + cross, 0.0) + EPS)

    logits_one = logits[:rows] * scale_one[:, :1]
    logits_two = (logits[:rows] + logits[rows:] * link[:, :1]) * scale_two[:, :1]
    powers_one, powers_two = jnp.exp(logits_one), jnp.exp(logits_two)
    logits[:rows] = powers_one
    logits[rows:] = powers_two
    columns = lax.broadcasted_iota(jnp.int32, (rows, vocab_own), 1) + at.mine * vocab_own

    def matches(i):
        return columns == marks[:, i : i + 1]

    parts = [
        powers_one,
        powers_two,
        powers_one * (logits_one * SHRINK),
        powers_two * (logits_two * SHRINK),
        powers_two * (logits_one * SHRINK),
        jnp.where(matches(0), logits_one, 0.0),
        jnp.where(matches(1), logits_two, 0.0),
        jnp.where(matches(1), logits_one, 0.0),
    ]
    lane = lax.broadcasted_iota(jnp.int32, (rows, LANES), 1)
    packed = jnp.zeros((rows, LANES), jnp.float32)
    for i, values in enumerate(parts):
        packed = jnp.where(lane == i, jnp.sum(values, axis=1, keepdims=True), packed)
    tall = stats.shape[1]
    packed = jnp.concatenate([packed, jnp.zeros((tall - rows, LANES), jnp.float32)], axis=0)
    stats[...] = packed.T[: stats.shape[0]]
    shared[at.mine] = stats[...]

    def share(k):
        q, target = at.other(k)
        return remote(stats, shared.at[at.mine], sems[30].at[q], sems[31].at[at.mine], target)

    def spread(k, _):
        share(k).start()
        return 0

    lax.fori_loop(1, blocks, spread, 0)

    def collect(k, _):
        q, target = at.other(k)
        remote(stats, shared.at[q], sems[30].at[q], sems[31].at[q], target).wait_recv()
        share(k).wait_send()
        return 0

    lax.fori_loop(1, blocks, collect, 0)
    table = jnp.sum(shared[...], axis=0)
    table = jnp.concatenate([table, jnp.zeros((LANES - table.shape[0], tall), jnp.float32)], axis=0)
    table = table.T[:rows]
    (totals_one, totals_two, mean_one, mean_two, mean_mixed, picked_one, picked_two, picked_mixed) = [
        table[:, i : i + 1] for i in range(8)
    ]

    weight_one, weight_two = usable_one, 0.8 * usable_two

    def gradient(powers, totals, i, weight):
        return (weight * (powers / totals - matches(i).astype(jnp.float32))).astype(jnp.bfloat16)

    dlogits[:rows] = gradient(logits[:rows], totals_one, 0, weight_one)
    dlogits[rows:] = gradient(logits[rows:], totals_two, 1, weight_two)
    link_back = later(link * scale_two)
    line = lax.broadcasted_iota(jnp.int32, (EXTRA, cols), 0)

    def part(q):
        grads = product(dlogits[...], w_lm[:, span(q)])
        one, two = grads[:rows], grads[rows:]
        here = scale_one[:, :1] * one + scale_two[:, :1] * two
        ahead = link_back[:, :1] * later(two) * level(q)
        gain_part = jnp.sum(
            feat_buf[q].astype(jnp.float32) * (here + 2.0 * ahead), axis=0, keepdims=True
        )
        return jnp.concatenate(
            [level(q) * (here + ahead), jnp.where(line == 0, gain_part, 0.0)], axis=0
        )

    def narrow(x):
        gain_row = x[rows : rows + 1]
        high = gain_row.astype(jnp.bfloat16).astype(jnp.float32)
        tail = jnp.where(line == 0, high, jnp.where(line == 1, gain_row - high, 0.0))
        return jnp.concatenate([x[:rows], tail], axis=0).astype(jnp.bfloat16)

    def widen(x):
        wide = x.astype(jnp.float32)
        gain_row = wide[rows : rows + 1] + wide[rows + 1 : rows + 2]
        return jnp.concatenate([wide[:rows], jnp.where(line == 0, gain_row, 0.0)], axis=0)

    scatter_sum(at, part, narrow, widen, buffers, sems[24:30], summed)

    def average(totals, picked, usable):
        count = jnp.sum(usable, axis=0, keepdims=True)
        return jnp.sum(usable * (jnp.log(totals) - picked), axis=0, keepdims=True) / jnp.maximum(
            count, 1.0
        )

    row = lax.broadcasted_iota(jnp.int32, losses.shape, 1)
    losses[...] = jnp.where(
        row == 0,
        average(totals_one, picked_one, usable_one),
        average(totals_two, picked_two, usable_two),
    )

    def wide(x):
        return jnp.broadcast_to(x, (rows, LANES))

    dot_one = wide(weight_one * (mean_one / (SHRINK * totals_one) - picked_one))
    dot_two = wide(weight_two * (mean_two / (SHRINK * totals_two) - picked_two))
    dot_mixed = wide(weight_two * (mean_mixed / (SHRINK * totals_two) - picked_mixed))
    pull_two = scale_two**3 * (dot_two / (scale_two * width))
    back_link = follows * (dot_two / scale_two - dot_mixed / scale_one) / width
    through = later(follows * (scale_two * back_link - pull_two * cross))
    pull_one = scale_one**3 * ((dot_one / width + through) / scale_one)

    gain = own_gain[...]
    state = feat_buf[at.mine].astype(jnp.float32)
    second = state + link[:, :1] * earlier(state * gain)
    pulled = later(second * (follows * pull_two)[:, :1]) * scale_one[:, :1]
    grad_state[...] = (
        summed[:rows] - gain * pulled - state * pull_one[:, :1] - second * pull_two[:, :1]
    ).astype(jnp.bfloat16)
    grad_gain[...] = summed[rows : rows + 1] - jnp.sum(pulled * state, axis=0, keepdims=True)


def whole_step(tensors, context, w_out, residual, fc_rest, w_fc, norm_gain, w_lm, marks, flags):
    rows = context.shape[0]
    width, cols = w_fc.shape
    vocab_own = w_lm.shape[1]
    blocks = 2 * tensors
    tall = -(-rows // LANES) * LANES
    far = pl.BlockSpec(memory_space=pl.ANY)
    return pl.pallas_call(
        functools.partial(step_kernel, tensors),
        out_shape=(
            jax.ShapeDtypeStruct((blocks, rows, cols), jnp.bfloat16),
            jax.ShapeDtypeStruct((rows, cols), jnp.bfloat16),
            jax.ShapeDtypeStruct((1, cols), jnp.float32),
            jax.ShapeDtypeStruct((1, LANES), jnp.float32),
        ),
        in_specs=[in_vmem()] * 7 + [far] * 2,
        out_specs=(in_vmem(),) * 4,
        scratch_shapes=[
            pltpu.VMEM((width, cols), jnp.bfloat16),
            pltpu.VMEM((vocab_own, width), jnp.bfloat16),
            pltpu.VMEM((rows, cols), jnp.float32),
            pltpu.VMEM((blocks, rows, cols), jnp.bfloat16),
            pltpu.VMEM((blocks, rows, cols), jnp.bfloat16),
            pltpu.VMEM((blocks, 8, cols), jnp.float32),
            pltpu.VMEM((3, rows, LANES), jnp.float32),
            pltpu.VMEM((2 * rows, vocab_own), jnp.float32),
            pltpu.VMEM((2 * rows, vocab_own), jnp.bfloat16),
            pltpu.VMEM((8, tall), jnp.float32),
            pltpu.VMEM((blocks, 8, tall), jnp.float32),
            pltpu.VMEM((rows + EXTRA, cols), jnp.float32),
            pltpu.SemaphoreType.DMA((2,)),
        ]
        + scatter_scratch(tensors, rows + EXTRA, cols)
        + gather_sems(tensors) * 3
        + scatter_sems(tensors) * 2
        + [pltpu.SemaphoreType.DMA((blocks,))] * 2,
        compiler_params=pltpu.CompilerParams(
            collective_id=0, has_side_effects=True, vmem_limit_bytes=VMEM_BYTES
        ),
    )(context, w_out, residual, fc_rest, norm_gain[None, :], marks, flags, w_fc, w_lm.T)


def on_device(
    context, w_out, residual, fc_rest, w_fc, norm_gain, w_lm, tokens, segments, vocab_map
):
    tensors = lax.axis_size("tensor")
    rows = tokens.shape[0] - 2
    width, cols = w_fc.shape
    seg_now = segments[:rows]
    follows = jnp.concatenate(
        [
            jnp.zeros((1,), jnp.float32),
            (segments[1:rows] == segments[: rows - 1]).astype(jnp.float32),
        ]
    )
    labels_all = vocab_map[tokens]
    labels = [labels_all[shift : shift + rows] for shift in (1, 2)]
    usable = [
        ((labels[k - 1] >= 0) & (segments[k : k + rows] == seg_now)).astype(jnp.float32)
        for k in (1, 2)
    ]
    captured, grad_state, grad_gain, losses = whole_step(
        tensors, context, w_out, residual, fc_rest, w_fc, norm_gain, w_lm,
        jnp.stack(labels, axis=1), jnp.stack([follows] + usable, axis=1),
    )
    grad_fc = (
        jnp.einsum("pti,tj->pij", captured, grad_state, preferred_element_type=jnp.float32)
        .astype(jnp.bfloat16)
        .reshape(width, cols)
    )
    return (losses[0, :2], grad_fc, grad_gain[0])


def solution(mesh):
    placed = (
        P("groups", ("tensor", "role")),
        P(("tensor", "role"), None),
        P("groups", ("tensor", "role")),
        P("groups", ("tensor", "role")),
        P(None, ("tensor", "role")),
        P(("tensor", "role")),
        P(None, ("tensor", "role")),
        P("groups"),
        P("groups"),
        P("groups"),
    )
    return jax.shard_map(
        on_device,
        mesh=mesh,
        in_specs=placed,
        out_specs=(P("groups"), P("groups", ("tensor", "role")), P(("groups", "tensor", "role"))),
        check_vma=False,
    )
```

```python
import functools

import jax
import jax.numpy as jnp
from jax import lax
from jax.experimental import pallas as pl
from jax.experimental.pallas import tpu as pltpu
from jax.sharding import PartitionSpec as P

EPS = 1e-05
SHRINK = 1.0 / 1024.0
VMEM_BYTES = 60 * 1024 * 1024
EXTRA = 16
LANES = 128
MESH = pl.DeviceIdType.MESH


def in_vmem():
    return pl.BlockSpec(memory_space=pltpu.VMEM)


def product(a, b):
    return jnp.dot(a, b, preferred_element_type=jnp.float32)


class Place:
    def __init__(self, tensors):
        self.lanes = 2 if tensors == 8 else 1
        self.depth = tensors // self.lanes
        self.tensors = tensors
        self.t, self.r = lax.axis_index("tensor"), lax.axis_index("role")
        self.z, self.y = self.t // self.lanes, lax.rem(self.t, self.lanes)
        self.mine = 2 * self.t + self.r

    def before(self, k):
        return lax.rem(self.z + self.depth - k, self.depth)

    def after(self, k):
        return lax.rem(self.z + k, self.depth)

    def across(self, z):
        return z * 2 + 1 - self.y

    def along(self, z):
        return z * self.lanes + self.y

    def other(self, k):
        q = lax.rem(self.mine + k, 2 * self.tensors)
        return q, {"tensor": q // 2, "role": lax.rem(q, 2)}

    def greet(self):
        barrier = pltpu.get_barrier_semaphore()
        others = 2 * self.tensors

        def hello(k, _):
            pl.semaphore_signal(barrier, inc=1, device_id=self.other(k)[1], device_id_type=MESH)
            return 0

        lax.fori_loop(1, others, hello, 0)
        pl.semaphore_wait(barrier, others - 1)


def remote(src, dst, send_sem, recv_sem, target):
    return pltpu.make_async_remote_copy(
        src_ref=src, dst_ref=dst, send_sem=send_sem, recv_sem=recv_sem,
        device_id=target, device_id_type=MESH,
    )


def scatter_scratch(tensors, rows, cols):
    depth = tensors // (2 if tensors == 8 else 1)
    return [pltpu.VMEM((tensors, rows, cols), jnp.float32)] * 2 + [
        pltpu.VMEM((depth, rows, cols), jnp.bfloat16)
    ] * 4


def scatter_sems(tensors):
    depth = tensors // (2 if tensors == 8 else 1)
    return [pltpu.SemaphoreType.DMA((tensors,))] * 2 + [pltpu.SemaphoreType.DMA((depth,))] * 4


def gather_sems(tensors):
    return [pltpu.SemaphoreType.DMA((tensors,))] * 6


def scatter_sum(at, part, narrow, widen, buffers, sems, total):
    height = total.shape[0]
    pair_out, pair_in, y_out, y_in, z_out, z_in = [b.at[:, pl.ds(0, height), :] for b in buffers]
    pair_send, pair_recv, y_send, y_recv, z_send, z_recv = sems
    depth, r = at.depth, at.r

    def pair(d):
        return remote(
            pair_out.at[d], pair_in.at[d], pair_send.at[d], pair_recv.at[d], {"role": 1 - r}
        )

    def cross(z):
        return remote(
            y_out.at[z], y_in.at[z], y_send.at[z], y_recv.at[z], {"tensor": at.across(at.z)}
        )

    def line(z):
        return remote(
            z_out.at[z], z_in.at[at.z], z_send.at[z], z_recv.at[at.z], {"tensor": at.along(z)}
        )

    def arrived(z):
        return remote(
            z_out.at[z], z_in.at[z], z_send.at[z], z_recv.at[z], {"tensor": at.along(z)}
        )

    def dests(z):
        return [at.across(z), at.along(z)] if at.lanes == 2 else [at.along(z)]

    def first(k):
        for d in dests(at.after(k)):
            pair_out[d] = part(2 * d + 1 - r)
            pair(d).start()

    def second(k):
        z = at.after(k)
        if at.lanes == 2:
            d = at.across(z)
            own = part(2 * d + r)
            pair(d).wait_recv()
            y_out[z] = narrow(own + pair_in[d])
            cross(z).start()
        d = at.along(z)
        own = part(2 * d + r)
        pair(d).wait_recv()
        pair_in[d] = own + pair_in[d]

    def merged(z):
        value = pair_in[at.along(z)]
        if at.lanes == 2:
            cross(z).wait_recv()
            value = value + widen(y_in[z])
        return value

    def third(k):
        z = at.after(k)
        z_out[z] = narrow(merged(z))
        line(z).start()

    first(1)
    if depth > 2:
        first(2)
    second(1)

    def step(k, _):
        first(k + 1)
        second(k)
        third(k - 1)
        return 0

    lax.fori_loop(2, depth, step, 0)
    if depth == 2:
        first(depth)
    second(depth)
    third(depth - 1)
    total[...] = merged(at.z)

    def collect(k, _):
        z = at.before(k)
        arrived(z).wait_recv()
        total[...] += widen(z_in[z])
        return 0

    lax.fori_loop(1, depth, collect, 0)

    def finish(k, _):
        z = at.after(k)
        line(z).wait_send()
        return 0

    def finish_near(k, _):
        z = at.after(k)
        for d in dests(z):
            pair(d).wait_send()
        if at.lanes == 2:
            cross(z).wait_send()
        return 0

    def drain():
        lax.fori_loop(1, depth, finish, 0)
        lax.fori_loop(0, depth, finish_near, 0)

    return drain


class Gather:
    def __init__(self, at, buf, sems, use):
        self.at, self.buf, self.sems, self.use = at, buf, sems, use

    def line(self, z):
        at, mine = self.at, self.buf.at[self.at.mine]
        return remote(
            mine, mine, self.sems[0].at[z], self.sems[1].at[at.z], {"tensor": at.along(z)}
        )

    def arrived(self, z):
        at = self.at
        block = self.buf.at[2 * at.along(z) + at.r]
        return remote(
            block, block, self.sems[0].at[z], self.sems[1].at[z], {"tensor": at.along(z)}
        )

    def cross(self, z, t):
        at = self.at
        block = self.buf.at[2 * t + at.r]
        return remote(
            block, block, self.sems[2].at[z], self.sems[3].at[z], {"tensor": at.across(at.z)}
        )

    def pair(self, t, r):
        block = self.buf.at[2 * t + r]
        return remote(
            block, block, self.sems[4].at[t], self.sems[5].at[t], {"role": 1 - self.at.r}
        )

    def start(self):
        at = self.at
        if at.lanes == 2:
            self.cross(at.z, at.t).start()

        def spread(k, _):
            self.line(at.after(k)).start()
            return 0

        lax.fori_loop(1, at.depth, spread, 0)
        self.pair(at.t, at.r).start()

    def over(self, k):
        at = self.at
        if at.lanes == 2:
            z = at.before(k)
            t = at.across(z)
            self.cross(z, t).wait_recv()
            self.pair(t, at.r).start()
            self.use(2 * t + at.r)

    def relay(self):
        at = self.at
        self.use(at.mine)

        def step(k, _):
            z = at.before(k)
            t = at.along(z)
            self.arrived(z).wait_recv()
            if at.lanes == 2:
                self.cross(z, t).start()
            self.pair(t, at.r).start()
            self.use(2 * t + at.r)
            self.over(k - 1)
            return 0

        lax.fori_loop(1, at.depth, step, 0)
        self.over(at.depth - 1)

    def finish(self):
        at = self.at

        def far(k, _):
            z = at.before(k)
            for t in [at.along(z)] + ([at.across(z)] if at.lanes == 2 else []):
                self.pair(t, 1 - at.r).wait_recv()
                self.use(2 * t + 1 - at.r)
            return 0

        lax.fori_loop(0, at.depth, far, 0)

    def drain(self):
        at = self.at

        def sent(k, _):
            z = at.after(k)
            self.pair(at.along(z), at.r).wait_send()
            if at.lanes == 2:
                self.cross(z, at.along(z)).wait_send()
                self.pair(at.across(z), at.r).wait_send()
            return 0

        lax.fori_loop(0, at.depth, sent, 0)

        def line_sent(k, _):
            self.line(at.after(k)).wait_send()
            return 0

        lax.fori_loop(1, at.depth, line_sent, 0)


def fold(x):
    total = x[:, :LANES]
    for start in range(LANES, x.shape[1], LANES):
        total = total + x[:, start : start + LANES]
    return total


def spread_sum(x):
    return jnp.broadcast_to(jnp.sum(x, axis=1, keepdims=True), x.shape)


def earlier(x):
    return pltpu.roll(x, 1, 0)


def later(x):
    return pltpu.roll(x, x.shape[0] - 1, 0)


def narrow_plain(x):
    return x.astype(jnp.bfloat16)


def widen_plain(x):
    return x.astype(jnp.float32)


def step_kernel(
    tensors, context, residual, fc_rest, own_gain, labels, segments, w_out_far, w_fc_far, w_lm_far,
    captured, grad_state, grad_gain, losses,
    w_out, w_fc, w_lm, total, cap_buf, feat_buf, gain_buf, moments, logits, dlogits, stats, shared,
    summed, notes, load, load_out, *scratch,
):
    at = Place(tensors)
    rows, cols = context.shape[0], w_fc.shape[1]
    width, vocab_own = w_fc.shape[0], w_lm.shape[0]
    blocks = 2 * tensors
    buffers, sems = scratch[:6], scratch[6:]
    load_fc = pltpu.make_async_copy(w_fc_far, w_fc, load.at[0])
    load_lm = pltpu.make_async_copy(w_lm_far, w_lm, load.at[1])

    def span(q):
        return pl.ds(pl.multiple_of(q * cols, cols), cols)

    def out_block(q):
        return pltpu.make_async_copy(
            w_out_far.at[:, span(q)], w_out.at[:, span(q)], load_out.at[q]
        )

    def fetch(k, _):
        z = at.after(k)
        order = [at.across(z), at.along(z)] if at.lanes == 2 else [at.along(z)]
        for d in order:
            out_block(2 * d + 1 - at.r).start()
        for d in order:
            out_block(2 * d + at.r).start()
        return 0

    lax.fori_loop(1, at.depth + 1, fetch, 0)
    load_fc.start()
    load_lm.start()
    gain_buf[at.mine] = jnp.broadcast_to(own_gain[...], gain_buf.shape[1:])
    at.greet()

    def level(q):
        return gain_buf[q][:1]

    def multiply(q):
        total[...] += product(cap_buf[q], w_fc[span(q), :])

    def head(q):
        state = feat_buf[q].astype(jnp.float32)
        scaled = state * level(q)
        before = earlier(scaled)
        moments[0] += fold(state * state)
        moments[1] += fold(state * before)
        moments[2] += fold(before * before)
        both = jnp.concatenate([scaled, before * level(q)], axis=0).astype(jnp.bfloat16)
        logits[...] += lax.dot_general(
            both, w_lm[:, span(q)], (((1,), (1,)), ((), ())), preferred_element_type=jnp.float32
        )

    gains = Gather(at, gain_buf, sems[0:6], lambda q: None)
    caps = Gather(at, cap_buf, sems[6:12], multiply)
    feats = Gather(at, feat_buf, sems[12:18], head)

    def first_part(q):
        out_block(q).wait()
        return product(context[...], w_out[:, span(q)])

    gains.start()
    drain_first = scatter_sum(
        at, first_part, narrow_plain, widen_plain,
        buffers, sems[18:24], total,
    )
    cap_buf[at.mine] = (total[...] + residual[...].astype(jnp.float32)).astype(jnp.bfloat16)
    caps.start()
    total[...] = fc_rest[...].astype(jnp.float32)
    moments[...] = jnp.zeros_like(moments)
    logits[...] = jnp.zeros_like(logits)
    notes[...] = jnp.zeros_like(notes)
    notes[0:1, : labels.shape[1]] = labels[...].astype(jnp.float32)
    notes[1:2, : labels.shape[1]] = segments[...].astype(jnp.float32)
    gains.relay()
    load_fc.wait()
    caps.relay()
    caps.finish()
    save = pltpu.make_async_copy(cap_buf, captured, load.at[2])
    save.start()
    feat_buf[at.mine] = total[...].astype(jnp.bfloat16)
    feats.start()
    gains.finish()
    load_lm.wait()
    columns_of = notes[...].T
    now = columns_of[:, 1:2]
    marks = [pltpu.roll(columns_of, columns_of.shape[0] - k, 0)[:rows] for k in (1, 2)]
    usable_one, usable_two = [
        jnp.where((mark[:, 0:1] >= 0.0) & (mark[:, 1:2] == now[:rows]), 1.0, 0.0) for mark in marks
    ]
    index = lax.broadcasted_iota(jnp.int32, (rows, 1), 0)
    same = (pltpu.roll(columns_of, 1, 0)[:rows, 1:2] == now[:rows]) & (index > 0)
    follows = jnp.broadcast_to(jnp.where(same, 1.0, 0.0), (rows, LANES))
    feats.relay()
    feats.finish()

    squares, mixed, squares_before = [spread_sum(moments[i]) / width for i in range(3)]
    scale_one = lax.rsqrt(squares + EPS)
    link = follows * earlier(scale_one)
    cross = link * (mixed + link * squares_before)
    scale_two = lax.rsqrt(jnp.maximum(squares + link * mixed + cross, 0.0) + EPS)

    logits_one = logits[:rows] * scale_one[:, :1]
    logits_two = (logits[:rows] + logits[rows:] * link[:, :1]) * scale_two[:, :1]
    powers_one, powers_two = jnp.exp(logits_one), jnp.exp(logits_two)
    logits[:rows] = powers_one
    logits[rows:] = powers_two
    columns = lax.broadcasted_iota(jnp.int32, (rows, vocab_own), 1) + at.mine * vocab_own

    def matches(i):
        return columns == marks[i][:, 0:1].astype(jnp.int32)

    parts = [
        powers_one,
        powers_two,
        powers_one * (logits_one * SHRINK),
        powers_two * (logits_two * SHRINK),
        powers_two * (logits_one * SHRINK),
        jnp.where(matches(0), logits_one, 0.0),
        jnp.where(matches(1), logits_two, 0.0),
        jnp.where(matches(1), logits_one, 0.0),
    ]
    lane = lax.broadcasted_iota(jnp.int32, (rows, LANES), 1)
    packed = jnp.zeros((rows, LANES), jnp.float32)
    for i, values in enumerate(parts):
        packed = jnp.where(lane == i, jnp.sum(values, axis=1, keepdims=True), packed)
    tall = stats.shape[1]
    packed = jnp.concatenate([packed, jnp.zeros((tall - rows, LANES), jnp.float32)], axis=0)
    stats[...] = packed.T[: stats.shape[0]]
    shared[at.mine] = stats[...]

    drain_first()

    def share(k):
        q, target = at.other(k)
        return remote(stats, shared.at[at.mine], sems[30].at[q], sems[31].at[at.mine], target)

    def spread(k, _):
        share(k).start()
        return 0

    lax.fori_loop(1, blocks, spread, 0)

    def collect(k, _):
        q, target = at.other(k)
        remote(stats, shared.at[q], sems[30].at[q], sems[31].at[q], target).wait_recv()
        share(k).wait_send()
        return 0

    lax.fori_loop(1, blocks, collect, 0)
    table = jnp.sum(shared[...], axis=0)
    table = jnp.concatenate([table, jnp.zeros((LANES - table.shape[0], tall), jnp.float32)], axis=0)
    table = table.T[:rows]
    (totals_one, totals_two, mean_one, mean_two, mean_mixed, picked_one, picked_two, picked_mixed) = [
        table[:, i : i + 1] for i in range(8)
    ]

    weight_one, weight_two = usable_one, 0.8 * usable_two

    def gradient(powers, totals, i, weight):
        return (weight * (powers / totals - matches(i).astype(jnp.float32))).astype(jnp.bfloat16)

    dlogits[:rows] = gradient(logits[:rows], totals_one, 0, weight_one)
    dlogits[rows:] = gradient(logits[rows:], totals_two, 1, weight_two)
    link_back = later(link * scale_two)
    line = lax.broadcasted_iota(jnp.int32, (EXTRA, cols), 0)

    def part(q):
        grads = product(dlogits[...], w_lm[:, span(q)])
        one, two = grads[:rows], grads[rows:]
        here = scale_one[:, :1] * one + scale_two[:, :1] * two
        ahead = link_back[:, :1] * later(two) * level(q)
        gain_part = jnp.sum(
            feat_buf[q].astype(jnp.float32) * (here + 2.0 * ahead), axis=0, keepdims=True
        )
        return jnp.concatenate(
            [level(q) * (here + ahead), jnp.where(line == 0, gain_part, 0.0)], axis=0
        )

    def narrow(x):
        gain_row = x[rows : rows + 1]
        high = gain_row.astype(jnp.bfloat16).astype(jnp.float32)
        tail = jnp.where(line == 0, high, jnp.where(line == 1, gain_row - high, 0.0))
        return jnp.concatenate([x[:rows], tail], axis=0).astype(jnp.bfloat16)

    def widen(x):
        wide = x.astype(jnp.float32)
        gain_row = wide[rows : rows + 1] + wide[rows + 1 : rows + 2]
        return jnp.concatenate([wide[:rows], jnp.where(line == 0, gain_row, 0.0)], axis=0)

    drain_second = scatter_sum(at, part, narrow, widen, buffers, sems[24:30], summed)

    def average(totals, picked, usable):
        count = jnp.sum(usable, axis=0, keepdims=True)
        return jnp.sum(usable * (jnp.log(totals) - picked), axis=0, keepdims=True) / jnp.maximum(
            count, 1.0
        )

    row = lax.broadcasted_iota(jnp.int32, losses.shape, 1)
    losses[...] = jnp.where(
        row == 0,
        average(totals_one, picked_one, usable_one),
        average(totals_two, picked_two, usable_two),
    )

    def wide(x):
        return jnp.broadcast_to(x, (rows, LANES))

    dot_one = wide(weight_one * (mean_one / (SHRINK * totals_one) - picked_one))
    dot_two = wide(weight_two * (mean_two / (SHRINK * totals_two) - picked_two))
    dot_mixed = wide(weight_two * (mean_mixed / (SHRINK * totals_two) - picked_mixed))
    pull_two = scale_two**3 * (dot_two / (scale_two * width))
    back_link = follows * (dot_two / scale_two - dot_mixed / scale_one) / width
    through = later(follows * (scale_two * back_link - pull_two * cross))
    pull_one = scale_one**3 * ((dot_one / width + through) / scale_one)

    gain = own_gain[...]
    state = feat_buf[at.mine].astype(jnp.float32)
    second = state + link[:, :1] * earlier(state * gain)
    pulled = later(second * (follows * pull_two)[:, :1]) * scale_one[:, :1]
    grad_state[...] = (
        summed[:rows] - gain * pulled - state * pull_one[:, :1] - second * pull_two[:, :1]
    ).astype(jnp.bfloat16)
    grad_gain[...] = summed[rows : rows + 1] - jnp.sum(pulled * state, axis=0, keepdims=True)
    drain_second()
    gains.drain()
    caps.drain()
    feats.drain()
    save.wait()


def whole_step(tensors, context, w_out, residual, fc_rest, w_fc, norm_gain, w_lm, labels, segments):
    rows = context.shape[0]
    width, cols = w_fc.shape
    vocab_own = w_lm.shape[1]
    blocks = 2 * tensors
    tall = -(-(rows + 2) // LANES) * LANES
    far = pl.BlockSpec(memory_space=pl.ANY)
    return pl.pallas_call(
        functools.partial(step_kernel, tensors),
        out_shape=(
            jax.ShapeDtypeStruct((blocks, rows, cols), jnp.bfloat16),
            jax.ShapeDtypeStruct((rows, cols), jnp.bfloat16),
            jax.ShapeDtypeStruct((1, cols), jnp.float32),
            jax.ShapeDtypeStruct((1, LANES), jnp.float32),
        ),
        in_specs=[in_vmem()] * 6 + [far] * 3,
        out_specs=(far,) + (in_vmem(),) * 3,
        scratch_shapes=[
            pltpu.VMEM(w_out.shape, jnp.bfloat16),
            pltpu.VMEM((width, cols), jnp.bfloat16),
            pltpu.VMEM((vocab_own, width), jnp.bfloat16),
            pltpu.VMEM((rows, cols), jnp.float32),
            pltpu.VMEM((blocks, rows, cols), jnp.bfloat16),
            pltpu.VMEM((blocks, rows, cols), jnp.bfloat16),
            pltpu.VMEM((blocks, 8, cols), jnp.float32),
            pltpu.VMEM((3, rows, LANES), jnp.float32),
            pltpu.VMEM((2 * rows, vocab_own), jnp.float32),
            pltpu.VMEM((2 * rows, vocab_own), jnp.bfloat16),
            pltpu.VMEM((8, tall), jnp.float32),
            pltpu.VMEM((blocks, 8, tall), jnp.float32),
            pltpu.VMEM((rows + EXTRA, cols), jnp.float32),
            pltpu.VMEM((LANES, tall), jnp.float32),
            pltpu.SemaphoreType.DMA((3,)),
            pltpu.SemaphoreType.DMA((blocks,)),
        ]
        + scatter_scratch(tensors, rows + EXTRA, cols)
        + gather_sems(tensors) * 3
        + scatter_sems(tensors) * 2
        + [pltpu.SemaphoreType.DMA((blocks,))] * 2,
        compiler_params=pltpu.CompilerParams(
            collective_id=0, has_side_effects=True, vmem_limit_bytes=VMEM_BYTES
        ),
    )(
        context, residual, fc_rest, norm_gain[None, :], labels[None, :], segments[None, :],
        w_out, w_fc, w_lm.T,
    )


def on_device(
    context, w_out, residual, fc_rest, w_fc, norm_gain, w_lm, tokens, segments, vocab_map
):
    tensors = lax.axis_size("tensor")
    width, cols = w_fc.shape
    captured, grad_state, grad_gain, losses = whole_step(
        tensors, context, w_out, residual, fc_rest, w_fc, norm_gain, w_lm,
        vocab_map[tokens], segments,
    )
    grad_fc = (
        jnp.einsum("pti,tj->pij", captured, grad_state, preferred_element_type=jnp.float32)
        .astype(jnp.bfloat16)
        .reshape(width, cols)
    )
    return (losses[0, :2], grad_fc, grad_gain[0])


def solution(mesh):
    placed = (
        P("groups", ("tensor", "role")),
        P(("tensor", "role"), None),
        P("groups", ("tensor", "role")),
        P("groups", ("tensor", "role")),
        P(None, ("tensor", "role")),
        P(("tensor", "role")),
        P(None, ("tensor", "role")),
        P("groups"),
        P("groups"),
        P("groups"),
    )
    return jax.shard_map(
        on_device,
        mesh=mesh,
        in_specs=placed,
        out_specs=(P("groups"), P("groups", ("tensor", "role")), P(("groups", "tensor", "role"))),
        check_vma=False,
    )
```

```python
import functools

import jax
import jax.numpy as jnp
from jax import lax
from jax.experimental import pallas as pl
from jax.experimental.pallas import tpu as pltpu
from jax.sharding import PartitionSpec as P

EPS = 1e-05
SHRINK = 1.0 / 1024.0
VMEM_BYTES = 60 * 1024 * 1024
EXTRA = 16
LANES = 128
MESH = pl.DeviceIdType.MESH


def in_vmem():
    return pl.BlockSpec(memory_space=pltpu.VMEM)


def product(a, b):
    return jnp.dot(a, b, preferred_element_type=jnp.float32)


class Place:
    def __init__(self, tensors):
        self.lanes = 2 if tensors == 8 else 1
        self.depth = tensors // self.lanes
        self.tensors = tensors
        self.t, self.r = lax.axis_index("tensor"), lax.axis_index("role")
        self.z, self.y = self.t // self.lanes, lax.rem(self.t, self.lanes)
        self.mine = 2 * self.t + self.r

    def before(self, k):
        return lax.rem(self.z + self.depth - k, self.depth)

    def after(self, k):
        return lax.rem(self.z + k, self.depth)

    def across(self, z):
        return z * 2 + 1 - self.y

    def along(self, z):
        return z * self.lanes + self.y

    def other(self, k):
        q = lax.rem(self.mine + k, 2 * self.tensors)
        return q, {"tensor": q // 2, "role": lax.rem(q, 2)}

    def greet(self):
        barrier = pltpu.get_barrier_semaphore()
        others = 2 * self.tensors

        def hello(k, _):
            pl.semaphore_signal(barrier, inc=1, device_id=self.other(k)[1], device_id_type=MESH)
            return 0

        lax.fori_loop(1, others, hello, 0)
        pl.semaphore_wait(barrier, others - 1)


def remote(src, dst, send_sem, recv_sem, target):
    return pltpu.make_async_remote_copy(
        src_ref=src, dst_ref=dst, send_sem=send_sem, recv_sem=recv_sem,
        device_id=target, device_id_type=MESH,
    )


def scatter_scratch(tensors, rows, cols):
    depth = tensors // (2 if tensors == 8 else 1)
    return [pltpu.VMEM((tensors, rows, cols), jnp.float32)] * 2 + [
        pltpu.VMEM((depth, rows, cols), jnp.bfloat16)
    ] * 4


def scatter_sems(tensors):
    depth = tensors // (2 if tensors == 8 else 1)
    return [pltpu.SemaphoreType.DMA((tensors,))] * 2 + [pltpu.SemaphoreType.DMA((depth,))] * 4


def gather_sems(tensors):
    return [pltpu.SemaphoreType.DMA((tensors,))] * 6


def scatter_sum(at, part, narrow, widen, buffers, sems, total):
    height = total.shape[0]
    pair_out, pair_in, y_out, y_in, z_out, z_in = [b.at[:, pl.ds(0, height), :] for b in buffers]
    pair_send, pair_recv, y_send, y_recv, z_send, z_recv = sems
    depth, r = at.depth, at.r

    def pair(d):
        return remote(
            pair_out.at[d], pair_in.at[d], pair_send.at[d], pair_recv.at[d], {"role": 1 - r}
        )

    def cross(z):
        return remote(
            y_out.at[z], y_in.at[z], y_send.at[z], y_recv.at[z], {"tensor": at.across(at.z)}
        )

    def line(z):
        return remote(
            z_out.at[z], z_in.at[at.z], z_send.at[z], z_recv.at[at.z], {"tensor": at.along(z)}
        )

    def arrived(z):
        return remote(
            z_out.at[z], z_in.at[z], z_send.at[z], z_recv.at[z], {"tensor": at.along(z)}
        )

    def dests(z):
        return [at.across(z), at.along(z)] if at.lanes == 2 else [at.along(z)]

    def first(k):
        for d in dests(at.after(k)):
            pair_out[d] = part(2 * d + 1 - r)
            pair(d).start()

    def second(k):
        z = at.after(k)
        if at.lanes == 2:
            d = at.across(z)
            own = part(2 * d + r)
            pair(d).wait_recv()
            y_out[z] = narrow(own + pair_in[d])
            cross(z).start()
        d = at.along(z)
        own = part(2 * d + r)
        pair(d).wait_recv()
        pair_in[d] = own + pair_in[d]

    def merged(z):
        value = pair_in[at.along(z)]
        if at.lanes == 2:
            cross(z).wait_recv()
            value = value + widen(y_in[z])
        return value

    def third(k):
        z = at.after(k)
        z_out[z] = narrow(merged(z))
        line(z).start()

    first(1)
    if depth > 2:
        first(2)
    second(1)

    def step(k, _):
        first(k + 1)
        second(k)
        third(k - 1)
        return 0

    lax.fori_loop(2, depth, step, 0)
    if depth == 2:
        first(depth)
    second(depth)
    third(depth - 1)
    total[...] = merged(at.z)

    def collect(k, _):
        z = at.before(k)
        arrived(z).wait_recv()
        total[...] += widen(z_in[z])
        return 0

    lax.fori_loop(1, depth, collect, 0)

    def finish(k, _):
        z = at.after(k)
        line(z).wait_send()
        return 0

    def finish_near(k, _):
        z = at.after(k)
        for d in dests(z):
            pair(d).wait_send()
        if at.lanes == 2:
            cross(z).wait_send()
        return 0

    def drain():
        lax.fori_loop(1, depth, finish, 0)
        lax.fori_loop(0, depth, finish_near, 0)

    return drain


class Gather:
    def __init__(self, at, buf, sems, use):
        self.at, self.buf, self.sems, self.use = at, buf, sems, use

    def line(self, z):
        at, mine = self.at, self.buf.at[self.at.mine]
        return remote(
            mine, mine, self.sems[0].at[z], self.sems[1].at[at.z], {"tensor": at.along(z)}
        )

    def arrived(self, z):
        at = self.at
        block = self.buf.at[2 * at.along(z) + at.r]
        return remote(
            block, block, self.sems[0].at[z], self.sems[1].at[z], {"tensor": at.along(z)}
        )

    def cross(self, z, t):
        at = self.at
        block = self.buf.at[2 * t + at.r]
        return remote(
            block, block, self.sems[2].at[z], self.sems[3].at[z], {"tensor": at.across(at.z)}
        )

    def pair(self, t, r):
        block = self.buf.at[2 * t + r]
        return remote(
            block, block, self.sems[4].at[t], self.sems[5].at[t], {"role": 1 - self.at.r}
        )

    def start(self):
        at = self.at
        if at.lanes == 2:
            self.cross(at.z, at.t).start()

        def spread(k, _):
            self.line(at.after(k)).start()
            return 0

        lax.fori_loop(1, at.depth, spread, 0)
        self.pair(at.t, at.r).start()

    def over(self, k):
        at = self.at
        if at.lanes == 2:
            z = at.before(k)
            t = at.across(z)
            self.cross(z, t).wait_recv()
            self.pair(t, at.r).start()
            self.use(2 * t + at.r)

    def relay(self):
        at = self.at
        self.use(at.mine)

        def step(k, _):
            z = at.before(k)
            t = at.along(z)
            self.arrived(z).wait_recv()
            if at.lanes == 2:
                self.cross(z, t).start()
            self.pair(t, at.r).start()
            self.use(2 * t + at.r)
            self.over(k - 1)
            return 0

        lax.fori_loop(1, at.depth, step, 0)
        self.over(at.depth - 1)

    def finish(self):
        at = self.at

        def far(k, _):
            z = at.before(k)
            for t in [at.along(z)] + ([at.across(z)] if at.lanes == 2 else []):
                self.pair(t, 1 - at.r).wait_recv()
                self.use(2 * t + 1 - at.r)
            return 0

        lax.fori_loop(0, at.depth, far, 0)

    def drain(self):
        at = self.at

        def sent(k, _):
            z = at.after(k)
            self.pair(at.along(z), at.r).wait_send()
            if at.lanes == 2:
                self.cross(z, at.along(z)).wait_send()
                self.pair(at.across(z), at.r).wait_send()
            return 0

        lax.fori_loop(0, at.depth, sent, 0)

        def line_sent(k, _):
            self.line(at.after(k)).wait_send()
            return 0

        lax.fori_loop(1, at.depth, line_sent, 0)


def fold(x):
    total = x[:, :LANES]
    for start in range(LANES, x.shape[1], LANES):
        total = total + x[:, start : start + LANES]
    return total


def spread_sum(x):
    return jnp.broadcast_to(jnp.sum(x, axis=1, keepdims=True), x.shape)


def earlier(x):
    return pltpu.roll(x, 1, 0)


def later(x):
    return pltpu.roll(x, x.shape[0] - 1, 0)


def narrow_plain(x):
    return x.astype(jnp.bfloat16)


def widen_plain(x):
    return x.astype(jnp.float32)


def step_kernel(
    tensors, context, residual, fc_rest, own_gain, labels, segments, w_out_far, w_fc_far, w_lm_far,
    captured, grad_state, grad_gain, losses,
    w_out, w_fc, w_lm, total, cap_buf, feat_buf, gain_buf, moments, logits, dlogits, stats, shared,
    summed, notes, load, load_out, *scratch,
):
    at = Place(tensors)
    rows, cols = context.shape[0], w_fc.shape[1]
    width, vocab_own = w_fc.shape[0], w_lm.shape[0]
    blocks = 2 * tensors
    buffers, sems = scratch[:6], scratch[6:]
    load_fc = pltpu.make_async_copy(w_fc_far, w_fc, load.at[0])
    load_lm = pltpu.make_async_copy(w_lm_far, w_lm, load.at[1])

    def span(q):
        return pl.ds(pl.multiple_of(q * cols, cols), cols)

    def out_block(q):
        return pltpu.make_async_copy(
            w_out_far.at[:, span(q)], w_out.at[:, span(q)], load_out.at[q]
        )

    def fetch(k, _):
        z = at.after(k)
        order = [at.across(z), at.along(z)] if at.lanes == 2 else [at.along(z)]
        for d in order:
            out_block(2 * d + 1 - at.r).start()
        for d in order:
            out_block(2 * d + at.r).start()
        return 0

    lax.fori_loop(1, at.depth + 1, fetch, 0)
    gain_buf[at.mine] = jnp.broadcast_to(own_gain[...], gain_buf.shape[1:])
    at.greet()
    load_fc.start()

    def level(q):
        return gain_buf[q][:1]

    def multiply(q):
        total[...] += product(cap_buf[q], w_fc[span(q), :])

    def head(q):
        state = feat_buf[q].astype(jnp.float32)
        scaled = state * level(q)
        before = earlier(scaled)
        moments[0] += fold(state * state)
        moments[1] += fold(state * before)
        moments[2] += fold(before * before)
        both = jnp.concatenate([scaled, before * level(q)], axis=0).astype(jnp.bfloat16)
        logits[...] += lax.dot_general(
            both, w_lm[:, span(q)], (((1,), (1,)), ((), ())), preferred_element_type=jnp.float32
        )

    gains = Gather(at, gain_buf, sems[0:6], lambda q: None)
    caps = Gather(at, cap_buf, sems[6:12], multiply)
    feats = Gather(at, feat_buf, sems[12:18], head)

    def first_part(q):
        out_block(q).wait()
        return product(context[...], w_out[:, span(q)])

    gains.start()
    drain_first = scatter_sum(
        at, first_part, narrow_plain, widen_plain,
        buffers, sems[18:24], total,
    )
    cap_buf[at.mine] = (total[...] + residual[...].astype(jnp.float32)).astype(jnp.bfloat16)
    caps.start()
    load_lm.start()
    total[...] = fc_rest[...].astype(jnp.float32)
    moments[...] = jnp.zeros_like(moments)
    logits[...] = jnp.zeros_like(logits)
    notes[...] = jnp.zeros_like(notes)
    notes[0:1, : labels.shape[1]] = labels[...].astype(jnp.float32)
    notes[1:2, : labels.shape[1]] = segments[...].astype(jnp.float32)
    gains.relay()
    load_fc.wait()
    caps.relay()
    caps.finish()
    save = pltpu.make_async_copy(cap_buf, captured, load.at[2])
    save.start()
    feat_buf[at.mine] = total[...].astype(jnp.bfloat16)
    feats.start()
    gains.finish()
    load_lm.wait()
    columns_of = notes[...].T
    now = columns_of[:, 1:2]
    marks = [pltpu.roll(columns_of, columns_of.shape[0] - k, 0)[:rows] for k in (1, 2)]
    usable_one, usable_two = [
        jnp.where((mark[:, 0:1] >= 0.0) & (mark[:, 1:2] == now[:rows]), 1.0, 0.0) for mark in marks
    ]
    index = lax.broadcasted_iota(jnp.int32, (rows, 1), 0)
    same = (pltpu.roll(columns_of, 1, 0)[:rows, 1:2] == now[:rows]) & (index > 0)
    follows = jnp.broadcast_to(jnp.where(same, 1.0, 0.0), (rows, LANES))
    feats.relay()
    feats.finish()

    squares, mixed, squares_before = [spread_sum(moments[i]) / width for i in range(3)]
    scale_one = lax.rsqrt(squares + EPS)
    link = follows * earlier(scale_one)
    cross = link * (mixed + link * squares_before)
    scale_two = lax.rsqrt(jnp.maximum(squares + link * mixed + cross, 0.0) + EPS)

    logits_one = logits[:rows] * scale_one[:, :1]
    logits_two = (logits[:rows] + logits[rows:] * link[:, :1]) * scale_two[:, :1]
    powers_one, powers_two = jnp.exp(logits_one), jnp.exp(logits_two)
    logits[:rows] = powers_one
    logits[rows:] = powers_two
    columns = lax.broadcasted_iota(jnp.int32, (rows, vocab_own), 1) + at.mine * vocab_own

    def matches(i):
        return columns == marks[i][:, 0:1].astype(jnp.int32)

    parts = [
        powers_one,
        powers_two,
        powers_one * (logits_one * SHRINK),
        powers_two * (logits_two * SHRINK),
        powers_two * (logits_one * SHRINK),
        jnp.where(matches(0), logits_one, 0.0),
        jnp.where(matches(1), logits_two, 0.0),
        jnp.where(matches(1), logits_one, 0.0),
    ]
    lane = lax.broadcasted_iota(jnp.int32, (rows, LANES), 1)
    packed = jnp.zeros((rows, LANES), jnp.float32)
    for i, values in enumerate(parts):
        packed = jnp.where(lane == i, jnp.sum(values, axis=1, keepdims=True), packed)
    tall = stats.shape[1]
    packed = jnp.concatenate([packed, jnp.zeros((tall - rows, LANES), jnp.float32)], axis=0)
    stats[...] = packed.T[: stats.shape[0]]
    shared[at.mine] = stats[...]

    drain_first()

    def share(k):
        q, target = at.other(k)
        return remote(stats, shared.at[at.mine], sems[30].at[q], sems[31].at[at.mine], target)

    def spread(k, _):
        share(k).start()
        return 0

    lax.fori_loop(1, blocks, spread, 0)

    def collect(k, _):
        q, target = at.other(k)
        remote(stats, shared.at[q], sems[30].at[q], sems[31].at[q], target).wait_recv()
        share(k).wait_send()
        return 0

    lax.fori_loop(1, blocks, collect, 0)
    table = jnp.sum(shared[...], axis=0)
    table = jnp.concatenate([table, jnp.zeros((LANES - table.shape[0], tall), jnp.float32)], axis=0)
    table = table.T[:rows]
    (totals_one, totals_two, mean_one, mean_two, mean_mixed, picked_one, picked_two, picked_mixed) = [
        table[:, i : i + 1] for i in range(8)
    ]

    weight_one, weight_two = usable_one, 0.8 * usable_two

    def gradient(powers, totals, i, weight):
        return (weight * (powers / totals - matches(i).astype(jnp.float32))).astype(jnp.bfloat16)

    dlogits[:rows] = gradient(logits[:rows], totals_one, 0, weight_one)
    dlogits[rows:] = gradient(logits[rows:], totals_two, 1, weight_two)
    link_back = later(link * scale_two)
    line = lax.broadcasted_iota(jnp.int32, (EXTRA, cols), 0)

    def part(q):
        grads = product(dlogits[...], w_lm[:, span(q)])
        one, two = grads[:rows], grads[rows:]
        here = scale_one[:, :1] * one + scale_two[:, :1] * two
        ahead = link_back[:, :1] * later(two) * level(q)
        gain_part = jnp.sum(
            feat_buf[q].astype(jnp.float32) * (here + 2.0 * ahead), axis=0, keepdims=True
        )
        return jnp.concatenate(
            [level(q) * (here + ahead), jnp.where(line == 0, gain_part, 0.0)], axis=0
        )

    def narrow(x):
        gain_row = x[rows : rows + 1]
        high = gain_row.astype(jnp.bfloat16).astype(jnp.float32)
        tail = jnp.where(line == 0, high, jnp.where(line == 1, gain_row - high, 0.0))
        return jnp.concatenate([x[:rows], tail], axis=0).astype(jnp.bfloat16)

    def widen(x):
        wide = x.astype(jnp.float32)
        gain_row = wide[rows : rows + 1] + wide[rows + 1 : rows + 2]
        return jnp.concatenate([wide[:rows], jnp.where(line == 0, gain_row, 0.0)], axis=0)

    drain_second = scatter_sum(at, part, narrow, widen, buffers, sems[24:30], summed)

    def average(totals, picked, usable):
        count = jnp.sum(usable, axis=0, keepdims=True)
        return jnp.sum(usable * (jnp.log(totals) - picked), axis=0, keepdims=True) / jnp.maximum(
            count, 1.0
        )

    row = lax.broadcasted_iota(jnp.int32, losses.shape, 1)
    losses[...] = jnp.where(
        row == 0,
        average(totals_one, picked_one, usable_one),
        average(totals_two, picked_two, usable_two),
    )

    def wide(x):
        return jnp.broadcast_to(x, (rows, LANES))

    dot_one = wide(weight_one * (mean_one / (SHRINK * totals_one) - picked_one))
    dot_two = wide(weight_two * (mean_two / (SHRINK * totals_two) - picked_two))
    dot_mixed = wide(weight_two * (mean_mixed / (SHRINK * totals_two) - picked_mixed))
    pull_two = scale_two**3 * (dot_two / (scale_two * width))
    back_link = follows * (dot_two / scale_two - dot_mixed / scale_one) / width
    through = later(follows * (scale_two * back_link - pull_two * cross))
    pull_one = scale_one**3 * ((dot_one / width + through) / scale_one)

    gain = own_gain[...]
    state = feat_buf[at.mine].astype(jnp.float32)
    second = state + link[:, :1] * earlier(state * gain)
    pulled = later(second * (follows * pull_two)[:, :1]) * scale_one[:, :1]
    grad_state[...] = (
        summed[:rows] - gain * pulled - state * pull_one[:, :1] - second * pull_two[:, :1]
    ).astype(jnp.bfloat16)
    grad_gain[...] = summed[rows : rows + 1] - jnp.sum(pulled * state, axis=0, keepdims=True)
    drain_second()
    gains.drain()
    caps.drain()
    feats.drain()
    save.wait()


def whole_step(tensors, context, w_out, residual, fc_rest, w_fc, norm_gain, w_lm, labels, segments):
    rows = context.shape[0]
    width, cols = w_fc.shape
    vocab_own = w_lm.shape[1]
    blocks = 2 * tensors
    tall = -(-(rows + 2) // LANES) * LANES
    far = pl.BlockSpec(memory_space=pl.ANY)
    return pl.pallas_call(
        functools.partial(step_kernel, tensors),
        out_shape=(
            jax.ShapeDtypeStruct((blocks, rows, cols), jnp.bfloat16),
            jax.ShapeDtypeStruct((rows, cols), jnp.bfloat16),
            jax.ShapeDtypeStruct((1, cols), jnp.float32),
            jax.ShapeDtypeStruct((1, 2), jnp.float32),
        ),
        in_specs=[in_vmem()] * 6 + [far] * 3,
        out_specs=(far,) + (in_vmem(),) * 3,
        scratch_shapes=[
            pltpu.VMEM(w_out.shape, jnp.bfloat16),
            pltpu.VMEM((width, cols), jnp.bfloat16),
            pltpu.VMEM((vocab_own, width), jnp.bfloat16),
            pltpu.VMEM((rows, cols), jnp.float32),
            pltpu.VMEM((blocks, rows, cols), jnp.bfloat16),
            pltpu.VMEM((blocks, rows, cols), jnp.bfloat16),
            pltpu.VMEM((blocks, 8, cols), jnp.float32),
            pltpu.VMEM((3, rows, LANES), jnp.float32),
            pltpu.VMEM((2 * rows, vocab_own), jnp.float32),
            pltpu.VMEM((2 * rows, vocab_own), jnp.bfloat16),
            pltpu.VMEM((8, tall), jnp.float32),
            pltpu.VMEM((blocks, 8, tall), jnp.float32),
            pltpu.VMEM((rows + EXTRA, cols), jnp.float32),
            pltpu.VMEM((LANES, tall), jnp.float32),
            pltpu.SemaphoreType.DMA((3,)),
            pltpu.SemaphoreType.DMA((blocks,)),
        ]
        + scatter_scratch(tensors, rows + EXTRA, cols)
        + gather_sems(tensors) * 3
        + scatter_sems(tensors) * 2
        + [pltpu.SemaphoreType.DMA((blocks,))] * 2,
        compiler_params=pltpu.CompilerParams(
            collective_id=0, has_side_effects=True, vmem_limit_bytes=VMEM_BYTES
        ),
    )(
        context, residual, fc_rest, norm_gain[None, :], labels[None, :], segments[None, :],
        w_out, w_fc, w_lm.T,
    )


def on_device(
    context, w_out, residual, fc_rest, w_fc, norm_gain, w_lm, tokens, segments, vocab_map
):
    tensors = lax.axis_size("tensor")
    width, cols = w_fc.shape
    captured, grad_state, grad_gain, losses = whole_step(
        tensors, context, w_out, residual, fc_rest, w_fc, norm_gain, w_lm,
        vocab_map[tokens], segments,
    )
    grad_fc = (
        jnp.einsum("pti,tj->pij", captured, grad_state, preferred_element_type=jnp.float32)
        .astype(jnp.bfloat16)
        .reshape(width, cols)
    )
    return (losses[0], grad_fc, grad_gain[0])


def solution(mesh):
    placed = (
        P("groups", ("tensor", "role")),
        P(("tensor", "role"), None),
        P("groups", ("tensor", "role")),
        P("groups", ("tensor", "role")),
        P(None, ("tensor", "role")),
        P(("tensor", "role")),
        P(None, ("tensor", "role")),
        P("groups"),
        P("groups"),
        P("groups"),
    )
    return jax.shard_map(
        on_device,
        mesh=mesh,
        in_specs=placed,
        out_specs=(P("groups"), P("groups", ("tensor", "role")), P(("groups", "tensor", "role"))),
        check_vma=False,
    )
```
